512 devices in a mesh: prefix: 8 (over x, core), branch: 32 (over z_lo, y), tensor: 2 (over z_hi).
Axes of the slice: x: 4, y: 4, z: 16 (z_hi: 2, z_lo: 8; z = z_hi * 8 + z_lo), core: 2. Of those that a mesh axis runs over, the one named last changes fastest.
Arguments:
- queries: bfloat16 [256, 128, 2048], P(('prefix', 'branch'), None, 'tensor'), may hold values from -16 to 16
- branch_keys: bfloat16 [256, 128, 512], P(('prefix', 'branch'), None, 'tensor'), may hold values from -4.5 to 4.5
- branch_values: bfloat16 [256, 128, 512], P(('prefix', 'branch'), None, 'tensor'), may hold values from -4.5 to 4.5
- grad_out: bfloat16 [256, 128, 2048], P(('prefix', 'branch'), None, 'tensor'), may hold values from -4.5 to 4.5
- prefix_keys: bfloat16 [2, 1024, 512], P(None, 'prefix', 'tensor'), may hold values from -16 to 16
- prefix_values: bfloat16 [2, 1024, 512], P(None, 'prefix', 'tensor'), may hold values from -4.5 to 4.5
- branch_prefix: int32 [256], P(('prefix', 'branch')), may hold values from 0 to 1
- branch_blocks: int32 [256], P(('prefix', 'branch')), may hold values from 1 to 1, as said below
Outputs:
- grad_queries: bfloat16 [256, 128, 2048], P(('prefix', 'branch'), None, 'tensor')
- grad_branch_keys: bfloat16 [256, 128, 512], P(('prefix', 'branch'), None, 'tensor')
- grad_branch_values: bfloat16 [256, 128, 512], P(('prefix', 'branch'), None, 'tensor')
- grad_prefix_keys: bfloat16 [2, 1024, 512], P(None, 'prefix', 'tensor')
- grad_prefix_values: bfloat16 [2, 1024, 512], P(None, 'prefix', 'tensor')
The draws below stay inside these ranges and needn't reach their ends.
Inputs may be any that keep to these rules, and one draw needn't show every extreme that they name: Branch b continues prefix branch_prefix[b]. Branch b has 128 * branch_blocks[b] live tokens; some branch has the one block.
All inputs are finite; a program needn't handle non-finite values.
Results may differ from the reference program's by a relative error of at most 0.012.
The reference program's roundings to bfloat16 on the way count: a program that leaves them out, or rounds other values in their place, can miss the bound.
Values may be sent and summed in bfloat16 or wider, within the bound.
A program may use at most 64 MiB of HBM per device.

```python
import math
import jax
import jax.numpy as jnp
import numpy as np
from jax import lax

HEADS = 16
KV_HEADS = 4
HDIM = 128
BLK = 128
PREFIXES = 2
PLEN = 1024
BLEN = 128
NBLK = 1
BRANCHES = 256


def draw_prefix_keys(key, part):
    key = jax.random.fold_in(key, 11)
    sample_rows = jnp.clip(jax.random.normal(key, (PREFIXES, PLEN, KV_HEADS * HDIM), jnp.float32), -4.5, 4.5)
    return sample_rows.astype(jnp.bfloat16)


def draw_queries(key, part):
    key = jax.random.fold_in(key, 23)
    noise_key = jax.random.fold_in(key, 0)
    sample_rows = jnp.clip(jax.random.normal(noise_key, (BRANCHES, BLEN, HEADS * HDIM), jnp.float32), -4.5, 4.5)
    return sample_rows.astype(jnp.bfloat16)


def draw_branch_blocks(key, part):
    key = jax.random.fold_in(key, 37)
    count_key, place_key = jax.random.split(key)
    counts = jax.random.randint(count_key, (BRANCHES,), 1, NBLK + 1, jnp.int32)
    fullest = jax.random.randint(place_key, (), 0, BRANCHES, jnp.int32)
    return counts.at[fullest].set(NBLK)


def set_ends(drawn, key, least, high):
    longest = drawn.shape.index(max(drawn.shape))
    spots = []
    for shift in (0, 1):
        where = [jax.random.randint(jax.random.fold_in(key, axis), (), 0, length) for axis, length in enumerate(drawn.shape)]
        where[longest] = (where[longest] + shift) % drawn.shape[longest]
        spots.append(tuple(where))
    return drawn.at[spots[0]].set(least).at[spots[1]].set(high)


def block_scale(own_key, extent, cuts, smallest, top_value):
    def one(dim, shards_of):
        draws = jax.random.uniform(jax.random.fold_in(jax.random.fold_in(own_key, 6), dim), (shards_of,), jnp.float32, smallest / len(cuts), top_value / len(cuts))
        return jnp.repeat(jnp.exp(draws), extent[dim] // shards_of).reshape((-1,) + (1,) * (len(extent) - dim - 1))

    level = one(*cuts[0])
    for cut in cuts[1:]:
        level = level * one(*cut)
    return level


def rank_table(count, skew):
    portions = [(1 << 20) // math.isqrt(rank ** skew) + 1 for rank in range(1, count + 1)]
    scale = 1 + sum(portions) // (1 << 30)
    return np.cumsum(np.array([max(1, weight // scale) for weight in portions]))


def ranked_ids(key, dims, amount, slope):
    grid = rank_table(amount, slope)
    pick = jax.random.randint(jax.random.fold_in(key, 1), dims, 0, int(grid[amount - 1]))
    rank = jnp.searchsorted(jnp.asarray(grid, jnp.int32), pick, side="right")
    return jax.random.permutation(jax.random.fold_in(key, 2), amount)[rank].astype(jnp.int32)


def gaussian(key, dims, scale, reach, cuts=(), kind=jnp.bfloat16):
    level = block_scale(key, dims, cuts, -0.22, 0.18) if cuts else 1.0
    drawn = jax.random.normal(key, dims, jnp.float32) * scale * level
    return jnp.minimum(jnp.maximum(drawn, -reach), reach).astype(kind)


def setup_inputs(seed: int = 0) -> dict:
    seeds = jax.random.split(jax.random.key(seed), 9)
    return {
        "queries": draw_queries(jax.random.fold_in(seeds[8], 71), 0),
        "branch_keys": gaussian(seeds[1], (BRANCHES, BLEN, KV_HEADS * HDIM), 1.0, 4.5, ((0, 256), (2, 2))),
        "branch_values": gaussian(seeds[2], (BRANCHES, BLEN, KV_HEADS * HDIM), 1.0, 4.5, ((0, 256), (2, 2))),
        "grad_out": gaussian(seeds[3], (BRANCHES, BLEN, HEADS * HDIM), 1.0, 4.5, ((0, 256), (2, 2))),
        "prefix_keys": draw_prefix_keys(jax.random.fold_in(seeds[8], 71), 0),
        "prefix_values": gaussian(seeds[5], (PREFIXES, PLEN, KV_HEADS * HDIM), 1.0, 4.5, ((1, 8), (2, 2))),
        "branch_prefix": set_ends(ranked_ids(seeds[6], (BRANCHES,), PREFIXES, 2), jax.random.fold_in(seeds[6], 3), 0, PREFIXES - 1).astype(jnp.int32),
        "branch_blocks": draw_branch_blocks(jax.random.fold_in(seeds[8], 71), 0),
    }


def branch_pass(query_rows, key_rows, value_rows, grad_rows, block_count):
    key_total = key_rows.shape[0]
    group_size = HEADS // KV_HEADS
    kv_owner = jnp.arange(HEADS) // group_size
    score_scale = 1.0 / math.sqrt(HDIM)
    query_wide = query_rows.astype(jnp.float32).reshape(BLEN, HEADS, HDIM)
    key_wide = key_rows.astype(jnp.float32).reshape(key_total, KV_HEADS, HDIM)[:, kv_owner, :]
    value_wide = value_rows.astype(jnp.float32).reshape(key_total, KV_HEADS, HDIM)[:, kv_owner, :]
    positions = jnp.arange(BLEN)
    columns = jnp.arange(key_total)
    allowed = (columns[None, :] < PLEN) | (columns[None, :] - PLEN <= positions[:, None])
    live_rows = positions < block_count * BLK
    grad_live = jnp.where(live_rows[:, None], grad_rows, jnp.zeros_like(grad_rows))
    grad_wide = grad_live.astype(jnp.float32).reshape(BLEN, HEADS, HDIM)
    scores = jnp.einsum('ihd,jhd->hij', query_wide, key_wide) * score_scale
    scores = jnp.where(allowed[None], scores, -1e+30)
    row_peak = lax.optimization_barrier(jnp.max(scores, axis=-1, keepdims=True))
    log_total = row_peak + jnp.log(lax.optimization_barrier(jnp.sum(jnp.exp(scores - row_peak), axis=-1, keepdims=True)))
    attention = jnp.exp(scores - log_total)
    attention_low = lax.optimization_barrier(attention.astype(jnp.bfloat16)).astype(jnp.float32)
    output = jnp.einsum('hij,jhd->ihd', attention_low, value_wide)
    row_delta = lax.optimization_barrier(jnp.sum(grad_wide * output, axis=-1)).T
    grad_attention = jnp.einsum('ihd,jhd->hij', grad_wide, value_wide)
    grad_scores = (attention * (grad_attention - row_delta[:, :, None])).astype(jnp.bfloat16)
    grad_scores_wide = lax.optimization_barrier(grad_scores).astype(jnp.float32)
    grad_query = (jnp.einsum('hij,jhd->ihd', grad_scores_wide, key_wide) * score_scale).astype(jnp.bfloat16)
    key_heads = jnp.einsum('hij,ihd->jhd', grad_scores_wide, query_wide) * score_scale
    value_heads = jnp.einsum('hij,ihd->jhd', attention_low, grad_wide)
    key_grads = key_heads.reshape(key_total, KV_HEADS, group_size, HDIM).sum(axis=2).reshape(key_total, KV_HEADS * HDIM)
    value_grads = value_heads.reshape(key_total, KV_HEADS, group_size, HDIM).sum(axis=2).reshape(key_total, KV_HEADS * HDIM)
    return (grad_query.reshape(BLEN, HEADS * HDIM), key_grads, value_grads)

def reference(queries, branch_keys, branch_values, grad_out, prefix_keys, prefix_values, branch_prefix, branch_blocks):
    kv_width = KV_HEADS * HDIM

    def branch_step(running, inputs):
        key_sum, value_sum = running
        query_rows, key_part, value_part, grad_rows, prefix_owner, block_count = inputs
        prefix_key = lax.dynamic_index_in_dim(prefix_keys, prefix_owner, 0, keepdims=False)
        prefix_value = lax.dynamic_index_in_dim(prefix_values, prefix_owner, 0, keepdims=False)
        key_rows = jnp.concatenate([prefix_key, key_part], axis=0)
        value_rows = jnp.concatenate([prefix_value, value_part], axis=0)
        grad_query, key_grads, value_grads = branch_pass(query_rows, key_rows, value_rows, grad_rows, block_count)
        chosen = (jnp.arange(PREFIXES) == prefix_owner)[:, None, None]
        key_sum = key_sum + jnp.where(chosen, key_grads[None, :PLEN], 0.0)
        value_sum = value_sum + jnp.where(chosen, value_grads[None, :PLEN], 0.0)
        return ((key_sum, value_sum), (grad_query, key_grads[PLEN:].astype(jnp.bfloat16), value_grads[PLEN:].astype(jnp.bfloat16)))
    start = (jnp.zeros((PREFIXES, PLEN, kv_width), jnp.float32), jnp.zeros((PREFIXES, PLEN, kv_width), jnp.float32))
    sums, results = lax.scan(branch_step, start, (queries, branch_keys, branch_values, grad_out, branch_prefix, branch_blocks))
    key_sum, value_sum = sums
    grad_queries, grad_branch_keys, grad_branch_values = results
    return (grad_queries, grad_branch_keys, grad_branch_values, key_sum.astype(jnp.bfloat16), value_sum.astype(jnp.bfloat16))
```

```python
import math

import jax
import jax.numpy as jnp
from jax import lax
from jax.experimental import pallas as pl
from jax.experimental.pallas import tpu as pltpu
from jax.sharding import PartitionSpec as P

HDIM = 128
BLK = 128
NX = 4
NY = 4
NZ = 8
OWNERS = 2 * NX
GROUP = 4
SCALE = 1.0 / math.sqrt(HDIM)
SCALE2 = SCALE * math.log2(math.e)
MESH = pl.DeviceIdType.MESH

RELS = [(2, 0), (2, 1), (1, 0), (1, 1), (3, 0), (3, 1), (0, 1)]


def nt(a, b):
    return lax.dot_general(a, b, (((1,), (1,)), ((), ())), preferred_element_type=jnp.float32)


def tn(a, b):
    return lax.dot_general(a, b, (((0,), (0,)), ((), ())), preferred_element_type=jnp.float32)


def nn(a, b):
    return lax.dot_general(a, b, (((1,), (0,)), ((), ())), preferred_element_type=jnp.float32)


def fold(a, op):
    return op(a.reshape(a.shape[0] // 8, 8, a.shape[1]), axis=0)


def kernel(
    bp_ref,
    bb_ref,
    q_ref,
    bk_ref,
    bv_ref,
    do_ref,
    pk_ref,
    pv_ref,
    gq_ref,
    gbk_ref,
    gbv_ref,
    gpk_ref,
    gpv_ref,
    kv,
    keys,
    qs,
    dos,
    s_buf,
    dp_buf,
    p_buf,
    ds_buf,
    own,
    term,
    got,
    acc,
    ys,
    yr,
    zs,
    zr,
    fin,
    g_s,
    g_r,
    c_s,
    c_r,
    t_s,
    t_r,
    y_s,
    y_r,
    z_s,
    z_r,
    za_s,
    za_r,
    ya_s,
    ya_r,
):
    me = lax.axis_index("prefix")
    b = lax.axis_index("branch")
    x, c = me // 2, lax.rem(me, 2)
    z, y = b // NY, lax.rem(b, NY)

    def owner(dx, dc):
        return lax.rem(x - dx + NX, NX) * 2 + lax.rem(c + dc, 2)

    def at_owner(o):
        return {"prefix": o, "branch": b}

    def at_y(dy):
        return {"prefix": me, "branch": z * NY + lax.rem(y + dy, NY)}

    def at_z(dz):
        return {"prefix": me, "branch": lax.rem(z + dz, NZ) * NY + y}

    def send(src, dst, ss, rs, dev):
        cp = pltpu.make_async_remote_copy(
            src_ref=src, dst_ref=dst, send_sem=ss, recv_sem=rs, device_id=dev, device_id_type=MESH
        )
        cp.start()
        return cp

    barrier = pltpu.get_barrier_semaphore()
    peers = [at_owner(owner(dx, dc)) for dx, dc in RELS]
    peers += [at_y(d) for d in range(1, NY)] + [at_z(d) for d in range(1, NZ)]
    for dev in peers:
        pl.semaphore_signal(barrier, inc=1, device_id=dev, device_id_type=MESH)

    pid = bp_ref[0]
    rows = lax.broadcasted_iota(jnp.int32, (BLK, HDIM), 0)
    live = rows < bb_ref[0] * BLK
    for g in range(2):
        cols = pl.ds(g * HDIM, HDIM)
        kv[g, me, 0] = pk_ref[:, :, cols]
        kv[g, me, 1] = pv_ref[:, :, cols]
        for h in range(GROUP):
            wide = pl.ds((g * GROUP + h) * HDIM, HDIM)
            qs[g, pl.ds(h * BLK, BLK)] = q_ref[0, :, wide]
            grad = do_ref[0, :, wide]
            dos[g, pl.ds(h * BLK, BLK)] = jnp.where(live, grad, jnp.zeros_like(grad))
    pl.semaphore_wait(barrier, len(peers))

    copies = []
    gather = {}
    for g in range(2):
        for dx in (1, 3, 2):
            to = lax.rem(x + dx, NX) * 2 + c
            gather[g, dx] = send(kv.at[g, me], kv.at[g, me], g_s.at[g, dx], g_r.at[g, dx], at_owner(to))
        gather[g, 0] = send(kv.at[g, me], kv.at[g, me], c_s.at[g, 0], c_r.at[g, 0], at_owner(owner(0, 1)))
    copies += gather.values()

    def chosen(g, o):
        pair = [jnp.where(pid == 0, kv[g, o, kind, 0], kv[g, o, kind, 1]) for kind in range(2)]
        keys[o] = pair[0]
        return pair

    def scores(g, slot, k, v, peak):
        s = nt(k, qs[g])
        if slot is None:
            slot = OWNERS
            key = lax.broadcasted_iota(jnp.int32, s.shape, 0)
            query = lax.rem(lax.broadcasted_iota(jnp.int32, s.shape, 1), BLK)
            s = jnp.where(key <= query, s, -1e30)
        s_buf[slot] = s
        dp_buf[slot] = nt(v, dos[g])
        top = fold(s, jnp.max)
        return top if peak is None else jnp.maximum(peak, top)

    terms = {}
    for g in range(2):
        cols = pl.ds(g * HDIM, HDIM)
        peak = scores(g, None, bk_ref[0, :, cols], bv_ref[0, :, cols], None)
        peak = scores(g, me, *chosen(g, me), peak)
        passed = {}
        for dx in (1, 3, 2):
            gather[g, dx].wait_recv()
            o = owner(dx, 0)
            passed[dx] = send(kv.at[g, o], kv.at[g, o], c_s.at[g, dx], c_r.at[g, dx], at_owner(owner(0, 1)))
            peak = scores(g, o, *chosen(g, o), peak)
        for dx in (0, 1, 3, 2):
            (passed[dx] if dx else gather[g, 0]).wait_recv()
            o = owner(dx, 1)
            peak = scores(g, o, *chosen(g, o), peak)
        for dx in (1, 3, 2):
            passed[dx].wait_send()
        top = jnp.max(peak, axis=0, keepdims=True) * SCALE2

        def exps(i, total):
            e = jnp.exp2(s_buf[i] * SCALE2 - top)
            s_buf[i] = e
            return total + fold(e, jnp.sum)

        width = GROUP * BLK
        total = lax.fori_loop(0, OWNERS + 1, exps, jnp.zeros((8, width), jnp.float32))
        share = 1.0 / jnp.sum(total, axis=0, keepdims=True)

        def probs(i, total):
            p = s_buf[i] * share
            low = p.astype(jnp.bfloat16)
            s_buf[i] = p
            p_buf[i] = low
            return total + fold(low.astype(jnp.float32) * dp_buf[i], jnp.sum)

        total = lax.fori_loop(0, OWNERS + 1, probs, jnp.zeros((8, width), jnp.float32))
        delta = jnp.sum(total, axis=0, keepdims=True)

        def grads(i):
            ds = (s_buf[i] * (dp_buf[i] - delta)).astype(jnp.bfloat16)
            ds_buf[i] = ds
            return nn(ds, qs[g]) * SCALE, nn(p_buf[i], dos[g])

        for k, (dx, dc) in enumerate(RELS):
            o = owner(dx, dc)
            dk, dv = grads(o)
            term[g, k, 0:BLK] = dk.astype(jnp.bfloat16)
            term[g, k, BLK : 2 * BLK] = dv.astype(jnp.bfloat16)
            term[g, k, 2 * BLK : 2 * BLK + 16] = jnp.full((16, HDIM), pid, jnp.int32).astype(
                jnp.float32
            ).astype(jnp.bfloat16)
            terms[g, k] = send(term.at[g, k], got.at[g, k], t_s.at[g, k], t_r.at[g, k], at_owner(o))
        dk, dv = grads(me)
        own[g, 0:BLK] = dk
        own[g, BLK : 2 * BLK] = dv
        dk, dv = grads(OWNERS)
        gbk_ref[0, :, cols] = dk.astype(jnp.bfloat16)
        gbv_ref[0, :, cols] = dv.astype(jnp.bfloat16)
        dq = tn(keys[...].reshape(OWNERS * BLK, HDIM), ds_buf[0:OWNERS].reshape(OWNERS * BLK, width))
        dq = (dq + tn(bk_ref[0, :, cols], ds_buf[OWNERS])) * SCALE
        for h in range(GROUP):
            wide = pl.ds((g * GROUP + h) * HDIM, HDIM)
            gq_ref[0, :, wide] = dq[:, h * BLK : (h + 1) * BLK].T.astype(jnp.bfloat16)
    copies_sent = list(terms.values())

    along_y = {}
    for g in range(2):
        for k in range(len(RELS)):
            terms[g, k].wait_recv()
        for half in range(2):
            part = pl.ds(half * BLK, BLK)
            mine = own[g, part]
            sums = [jnp.where(pid == p, mine, 0.0) for p in range(2)]
            for k in range(len(RELS)):
                t = got[g, k, part].astype(jnp.float32)
                whose = got[g, k, 2 * BLK : 2 * BLK + 16].astype(jnp.float32)[0:1]
                first = jnp.broadcast_to(whose, t.shape) < 0.5
                sums[0] += jnp.where(first, t, 0.0)
                sums[1] += jnp.where(first, 0.0, t)
            for p in range(2):
                acc[g, p, half] = sums[p]
                for quarter in range(NY):
                    at = quarter * 32
                    ys[g, quarter, p, half] = sums[p][at : at + 32].astype(jnp.bfloat16)
        for dy in range(1, NY):
            along_y[g, dy] = send(
                ys.at[g, lax.rem(y + dy, NY)], yr.at[g, dy], y_s.at[g, dy], y_r.at[g, dy], at_y(dy)
            )
    copies_sent += along_y.values()

    along_z = {}
    for g in range(2):
        for dy in range(1, NY):
            along_y[g, dy].wait_recv()
        for p in range(2):
            for half in range(2):
                total = acc[g, p, half, pl.ds(y * 32, 32)]
                for dy in range(1, NY):
                    total += yr[g, dy, p, half].astype(jnp.float32)
                zs[g, 4 * p + 2 * half] = total[0:16]
                zs[g, 4 * p + 2 * half + 1] = total[16:32]
        for dz in range(1, NZ):
            along_z[g, dz] = send(
                zs.at[g, lax.rem(z + dz, NZ)], zr.at[g, dz], z_s.at[g, dz], z_r.at[g, dz], at_z(dz)
            )
    copies_sent += along_z.values()

    back_z = {}
    for g in range(2):
        total = zs[g, z]
        for dz in range(1, NZ):
            along_z[g, dz].wait_recv()
            total += zr[g, dz]
        fin[g, y, z] = total.astype(jnp.bfloat16)
        for dz in range(1, NZ):
            here = fin.at[g, y, z]
            back_z[g, dz] = send(here, here, za_s.at[g, dz], za_r.at[g, dz], at_z(dz))
    copies_sent += back_z.values()

    back_y = {}
    for g in range(2):
        for dz in range(1, NZ):
            back_z[g, dz].wait_recv()
        for dy in range(1, NY):
            here = fin.at[g, y]
            back_y[g, dy] = send(here, here, ya_s.at[g, dy], ya_r.at[g, dy], at_y(dy))
    copies_sent += back_y.values()

    for g in range(2):
        cols = pl.ds(g * HDIM, HDIM)
        for dy in range(1, NY):
            back_y[g, dy].wait_recv()
        for quarter in range(NY):
            for p in range(2):
                for low in range(2):
                    at = pl.ds(quarter * 32 + low * 16, 16)
                    gpk_ref[p, at, cols] = fin[g, quarter, 4 * p + low]
                    gpv_ref[p, at, cols] = fin[g, quarter, 4 * p + 2 + low]
    for cp in copies + copies_sent:
        cp.wait_send()


def body(queries, branch_keys, branch_values, grad_out, prefix_keys, prefix_values, branch_prefix, branch_blocks):
    bf16, f32 = jnp.bfloat16, jnp.float32
    vmem = pl.BlockSpec(memory_space=pltpu.VMEM)
    smem = pl.BlockSpec(memory_space=pltpu.SMEM)
    width = GROUP * BLK
    dma = pltpu.SemaphoreType.DMA
    return pl.pallas_call(
        kernel,
        out_shape=[
            jax.ShapeDtypeStruct(a.shape, bf16)
            for a in (queries, branch_keys, branch_values, prefix_keys, prefix_values)
        ],
        in_specs=[smem, smem] + [vmem] * 6,
        out_specs=[vmem] * 5,
        scratch_shapes=[
            pltpu.VMEM((2, OWNERS, 2, 2, BLK, HDIM), bf16),
            pltpu.VMEM((OWNERS, BLK, HDIM), bf16),
            pltpu.VMEM((2, width, HDIM), bf16),
            pltpu.VMEM((2, width, HDIM), bf16),
            pltpu.VMEM((OWNERS + 1, BLK, width), f32),
            pltpu.VMEM((OWNERS + 1, BLK, width), f32),
            pltpu.VMEM((OWNERS + 1, BLK, width), bf16),
            pltpu.VMEM((OWNERS + 1, BLK, width), bf16),
            pltpu.VMEM((2, 2 * BLK, HDIM), f32),
            pltpu.VMEM((2, 7, 2 * BLK + 16, HDIM), bf16),
            pltpu.VMEM((2, 7, 2 * BLK + 16, HDIM), bf16),
            pltpu.VMEM((2, 2, 2, BLK, HDIM), f32),
            pltpu.VMEM((2, NY, 2, 2, 32, HDIM), bf16),
            pltpu.VMEM((2, NY, 2, 2, 32, HDIM), bf16),
            pltpu.VMEM((2, NZ, 16, HDIM), f32),
            pltpu.VMEM((2, NZ, 16, HDIM), f32),
            pltpu.VMEM((2, NY, NZ, 16, HDIM), bf16),
        ]
        + [dma((2, NX))] * 4
        + [dma((2, 7))] * 2
        + [dma((2, NY))] * 2
        + [dma((2, NZ))] * 4
        + [dma((2, NY))] * 2,
        compiler_params=pltpu.CompilerParams(
            collective_id=0, has_side_effects=True, vmem_limit_bytes=40 << 20
        ),
        name="attention_backward",
    )(branch_prefix, branch_blocks, queries, branch_keys, branch_values, grad_out, prefix_keys, prefix_values)


def solution(mesh):
    split = P(("prefix", "branch"), None, "tensor")
    rows = P(None, "prefix", "tensor")
    ids = P(("prefix", "branch"))
    return jax.shard_map(
        body,
        mesh=mesh,
        in_specs=(split, split, split, split, rows, rows, ids, ids),
        out_specs=(split, split, split, rows, rows),
        check_vma=False,
    )
```

```python
import math

import jax
import jax.numpy as jnp
from jax import lax
from jax.experimental import pallas as pl
from jax.experimental.pallas import tpu as pltpu
from jax.sharding import PartitionSpec as P

HDIM = 128
BLK = 128
NX = 4
NY = 4
NZ = 8
OWNERS = 2 * NX
GROUP = 4
SCALE = 1.0 / math.sqrt(HDIM)
SCALE2 = SCALE * math.log2(math.e)
MESH = pl.DeviceIdType.MESH

RELS = [(2, 0), (2, 1), (1, 0), (1, 1), (3, 0), (3, 1), (0, 1)]


def nt(a, b):
    return lax.dot_general(a, b, (((1,), (1,)), ((), ())), preferred_element_type=jnp.float32)


def tn(a, b):
    return lax.dot_general(a, b, (((0,), (0,)), ((), ())), preferred_element_type=jnp.float32)


def nn(a, b):
    return lax.dot_general(a, b, (((1,), (0,)), ((), ())), preferred_element_type=jnp.float32)


def fold(a, op):
    return op(a.reshape(a.shape[0] // 8, 8, a.shape[1]), axis=0)


def kernel(
    bp_ref,
    bb_ref,
    q_hbm,
    bk_hbm,
    bv_hbm,
    do_hbm,
    pk_hbm,
    pv_hbm,
    gq_hbm,
    gbk_hbm,
    gbv_hbm,
    gpk_hbm,
    gpv_hbm,
    q_ref,
    bk_ref,
    bv_ref,
    do_ref,
    gq_ref,
    gbk_ref,
    gbv_ref,
    gpk_ref,
    gpv_ref,
    kv,
    keys,
    qs,
    dos,
    s_buf,
    dp_buf,
    p_buf,
    ds_buf,
    own,
    term,
    got,
    acc,
    ys,
    yr,
    zs,
    zr,
    fin,
    g_s,
    g_r,
    c_s,
    c_r,
    t_s,
    t_r,
    y_s,
    y_r,
    z_s,
    z_r,
    za_s,
    za_r,
    ya_s,
    ya_r,
    in_s,
    out_s,
):
    me = lax.axis_index("prefix")
    b = lax.axis_index("branch")
    x, c = me // 2, lax.rem(me, 2)
    z, y = b // NY, lax.rem(b, NY)

    def owner(dx, dc):
        return lax.rem(x - dx + NX, NX) * 2 + lax.rem(c + dc, 2)

    def at_owner(o):
        return {"prefix": o, "branch": b}

    def at_y(dy):
        return {"prefix": me, "branch": z * NY + lax.rem(y + dy, NY)}

    def at_z(dz):
        return {"prefix": me, "branch": lax.rem(z + dz, NZ) * NY + y}

    def send(src, dst, ss, rs, dev):
        cp = pltpu.make_async_remote_copy(
            src_ref=src, dst_ref=dst, send_sem=ss, recv_sem=rs, device_id=dev, device_id_type=MESH
        )
        cp.start()
        return cp

    def local(src, dst, sem):
        cp = pltpu.make_async_copy(src, dst, sem)
        cp.start()
        return cp

    prefix_in = []
    for g in range(2):
        for kind, ref in enumerate((pk_hbm, pv_hbm)):
            part = ref.at[:, :, pl.ds(g * HDIM, HDIM)]
            prefix_in.append(local(part, kv.at[g, me, kind], in_s.at[2 * g + kind]))
    branch_in = [
        local(src, dst, in_s.at[4 + i])
        for i, (src, dst) in enumerate(
            ((bk_hbm, bk_ref), (bv_hbm, bv_ref), (q_hbm, q_ref), (do_hbm, do_ref))
        )
    ]

    barrier = pltpu.get_barrier_semaphore()
    peers = [at_owner(owner(dx, dc)) for dx, dc in RELS]
    peers += [at_y(d) for d in range(1, NY)] + [at_z(d) for d in range(1, NZ)]
    for dev in peers:
        pl.semaphore_signal(barrier, inc=1, device_id=dev, device_id_type=MESH)

    pid = bp_ref[0]
    for cp in prefix_in:
        cp.wait()
    pl.semaphore_wait(barrier, len(peers))

    copies = []
    gather = {}
    for g in range(2):
        for dx in (1, 3, 2):
            to = lax.rem(x + dx, NX) * 2 + c
            gather[g, dx] = send(kv.at[g, me], kv.at[g, me], g_s.at[g, dx], g_r.at[g, dx], at_owner(to))
        gather[g, 0] = send(kv.at[g, me], kv.at[g, me], c_s.at[g, 0], c_r.at[g, 0], at_owner(owner(0, 1)))
    copies += gather.values()

    for cp in branch_in:
        cp.wait()
    live = lax.broadcasted_iota(jnp.int32, (BLK, HDIM), 0) < bb_ref[0] * BLK
    for g in range(2):
        for h in range(GROUP):
            wide = pl.ds((g * GROUP + h) * HDIM, HDIM)
            qs[g, pl.ds(h * BLK, BLK)] = q_ref[0, :, wide]
            grad = do_ref[0, :, wide]
            dos[g, pl.ds(h * BLK, BLK)] = jnp.where(live, grad, jnp.zeros_like(grad))

    def chosen(g, o):
        pair = [jnp.where(pid == 0, kv[g, o, kind, 0], kv[g, o, kind, 1]) for kind in range(2)]
        keys[o] = pair[0]
        return pair

    def scores(g, slot, k, v, peak):
        s = nt(k, qs[g])
        if slot is None:
            slot = OWNERS
            key = lax.broadcasted_iota(jnp.int32, s.shape, 0)
            query = lax.rem(lax.broadcasted_iota(jnp.int32, s.shape, 1), BLK)
            s = jnp.where(key <= query, s, -1e30)
        s_buf[slot] = s
        dp_buf[slot] = nt(v, dos[g])
        top = fold(s, jnp.max)
        return top if peak is None else jnp.maximum(peak, top)

    terms = {}
    for g in range(2):
        cols = pl.ds(g * HDIM, HDIM)
        peak = scores(g, None, bk_ref[0, :, cols], bv_ref[0, :, cols], None)
        peak = scores(g, me, *chosen(g, me), peak)
        passed = {}
        for dx in (1, 3, 2):
            gather[g, dx].wait_recv()
            o = owner(dx, 0)
            passed[dx] = send(kv.at[g, o], kv.at[g, o], c_s.at[g, dx], c_r.at[g, dx], at_owner(owner(0, 1)))
            peak = scores(g, o, *chosen(g, o), peak)
        for dx in (0, 1, 3, 2):
            (passed[dx] if dx else gather[g, 0]).wait_recv()
            o = owner(dx, 1)
            peak = scores(g, o, *chosen(g, o), peak)
        for dx in (1, 3, 2):
            passed[dx].wait_send()
        top = jnp.max(peak, axis=0, keepdims=True) * SCALE2

        def exps(i, total):
            e = jnp.exp2(s_buf[i] * SCALE2 - top)
            s_buf[i] = e
            return total + fold(e, jnp.sum)

        width = GROUP * BLK
        total = lax.fori_loop(0, OWNERS + 1, exps, jnp.zeros((8, width), jnp.float32))
        share = 1.0 / jnp.sum(total, axis=0, keepdims=True)

        def probs(i, total):
            p = s_buf[i] * share
            low = p.astype(jnp.bfloat16)
            s_buf[i] = p
            p_buf[i] = low
            return total + fold(low.astype(jnp.float32) * dp_buf[i], jnp.sum)

        total = lax.fori_loop(0, OWNERS + 1, probs, jnp.zeros((8, width), jnp.float32))
        delta = jnp.sum(total, axis=0, keepdims=True)

        def grads(i):
            ds = (s_buf[i] * (dp_buf[i] - delta)).astype(jnp.bfloat16)
            ds_buf[i] = ds
            return nn(ds, qs[g]) * SCALE, nn(p_buf[i], dos[g])

        for k, (dx, dc) in enumerate(RELS):
            o = owner(dx, dc)
            dk, dv = grads(o)
            term[g, k, 0:BLK] = dk.astype(jnp.bfloat16)
            term[g, k, BLK : 2 * BLK] = dv.astype(jnp.bfloat16)
            term[g, k, 2 * BLK : 2 * BLK + 16] = jnp.full((16, HDIM), pid, jnp.int32).astype(
                jnp.float32
            ).astype(jnp.bfloat16)
            terms[g, k] = send(term.at[g, k], got.at[g, k], t_s.at[g, k], t_r.at[g, k], at_owner(o))
        dk, dv = grads(me)
        own[g, 0:BLK] = dk
        own[g, BLK : 2 * BLK] = dv
        dk, dv = grads(OWNERS)
        gbk_ref[0, :, cols] = dk.astype(jnp.bfloat16)
        gbv_ref[0, :, cols] = dv.astype(jnp.bfloat16)
        dq = tn(keys[...].reshape(OWNERS * BLK, HDIM), ds_buf[0:OWNERS].reshape(OWNERS * BLK, width))
        dq = (dq + tn(bk_ref[0, :, cols], ds_buf[OWNERS])) * SCALE
        for h in range(GROUP):
            wide = pl.ds((g * GROUP + h) * HDIM, HDIM)
            gq_ref[0, :, wide] = dq[:, h * BLK : (h + 1) * BLK].T.astype(jnp.bfloat16)
    outs = [
        local(src, dst, out_s.at[i])
        for i, (src, dst) in enumerate(((gq_ref, gq_hbm), (gbk_ref, gbk_hbm), (gbv_ref, gbv_hbm)))
    ]
    copies_sent = list(terms.values())

    along_y = {}
    for g in range(2):
        for k in range(len(RELS)):
            terms[g, k].wait_recv()
        for half in range(2):
            part = pl.ds(half * BLK, BLK)
            mine = own[g, part]
            sums = [jnp.where(pid == p, mine, 0.0) for p in range(2)]
            for k in range(len(RELS)):
                t = got[g, k, part].astype(jnp.float32)
                whose = got[g, k, 2 * BLK : 2 * BLK + 16].astype(jnp.float32)[0:1]
                first = jnp.broadcast_to(whose, t.shape) < 0.5
                sums[0] += jnp.where(first, t, 0.0)
                sums[1] += jnp.where(first, 0.0, t)
            for p in range(2):
                acc[g, p, half] = sums[p]
                for quarter in range(NY):
                    at = quarter * 32
                    ys[g, quarter, p, half] = sums[p][at : at + 32].astype(jnp.bfloat16)
        for dy in range(1, NY):
            along_y[g, dy] = send(
                ys.at[g, lax.rem(y + dy, NY)], yr.at[g, dy], y_s.at[g, dy], y_r.at[g, dy], at_y(dy)
            )
    copies_sent += along_y.values()

    along_z = {}
    for g in range(2):
        for dy in range(1, NY):
            along_y[g, dy].wait_recv()
        for p in range(2):
            for half in range(2):
                total = acc[g, p, half, pl.ds(y * 32, 32)]
                for dy in range(1, NY):
                    total += yr[g, dy, p, half].astype(jnp.float32)
                zs[g, 4 * p + 2 * half] = total[0:16]
                zs[g, 4 * p + 2 * half + 1] = total[16:32]
        for dz in range(1, NZ):
            along_z[g, dz] = send(
                zs.at[g, lax.rem(z + dz, NZ)], zr.at[g, dz], z_s.at[g, dz], z_r.at[g, dz], at_z(dz)
            )
    copies_sent += along_z.values()

    back_z = {}
    for g in range(2):
        total = zs[g, z]
        for dz in range(1, NZ):
            along_z[g, dz].wait_recv()
            total += zr[g, dz]
        fin[g, y, z] = total.astype(jnp.bfloat16)
        for dz in range(1, NZ):
            here = fin.at[g, y, z]
            back_z[g, dz] = send(here, here, za_s.at[g, dz], za_r.at[g, dz], at_z(dz))
    copies_sent += back_z.values()

    back_y = {}
    for g in range(2):
        for dz in range(1, NZ):
            back_z[g, dz].wait_recv()
        for dy in range(1, NY):
            here = fin.at[g, y]
            back_y[g, dy] = send(here, here, ya_s.at[g, dy], ya_r.at[g, dy], at_y(dy))
    copies_sent += back_y.values()

    for g in range(2):
        cols = pl.ds(g * HDIM, HDIM)
        for dy in range(1, NY):
            back_y[g, dy].wait_recv()
        for quarter in range(NY):
            for p in range(2):
                for low in range(2):
                    at = pl.ds(quarter * 32 + low * 16, 16)
                    gpk_ref[p, at, cols] = fin[g, quarter, 4 * p + low]
                    gpv_ref[p, at, cols] = fin[g, quarter, 4 * p + 2 + low]
    outs += [local(gpk_ref, gpk_hbm, out_s.at[3]), local(gpv_ref, gpv_hbm, out_s.at[4])]
    for cp in copies + copies_sent:
        cp.wait_send()
    for cp in outs:
        cp.wait()


def hand_over(*refs):
    for i in range(5):
        refs[5 + i][...] = refs[i][...]


def body(queries, branch_keys, branch_values, grad_out, prefix_keys, prefix_values, branch_prefix, branch_blocks):
    bf16, f32 = jnp.bfloat16, jnp.float32
    smem = pl.BlockSpec(memory_space=pltpu.SMEM)
    hbm = pl.BlockSpec(memory_space=pltpu.HBM)
    anywhere = pl.BlockSpec(memory_space=pl.ANY)
    width = GROUP * BLK
    dma = pltpu.SemaphoreType.DMA
    shapes = [a.shape for a in (queries, branch_keys, branch_values, prefix_keys, prefix_values)]
    wide, narrow, _, prefix, _ = (pltpu.VMEM(shape, bf16) for shape in shapes)
    out_shape = [jax.ShapeDtypeStruct(shape, bf16) for shape in shapes]
    results = pl.pallas_call(
        kernel,
        out_shape=out_shape,
        in_specs=[smem, smem] + [hbm] * 6,
        out_specs=[anywhere] * 5,
        scratch_shapes=[
            wide,
            narrow,
            narrow,
            wide,
            wide,
            narrow,
            narrow,
            prefix,
            prefix,
            pltpu.VMEM((2, OWNERS, 2, 2, BLK, HDIM), bf16),
            pltpu.VMEM((OWNERS, BLK, HDIM), bf16),
            pltpu.VMEM((2, width, HDIM), bf16),
            pltpu.VMEM((2, width, HDIM), bf16),
            pltpu.VMEM((OWNERS + 1, BLK, width), f32),
            pltpu.VMEM((OWNERS + 1, BLK, width), f32),
            pltpu.VMEM((OWNERS + 1, BLK, width), bf16),
            pltpu.VMEM((OWNERS + 1, BLK, width), bf16),
            pltpu.VMEM((2, 2 * BLK, HDIM), f32),
            pltpu.VMEM((2, 7, 2 * BLK + 16, HDIM), bf16),
            pltpu.VMEM((2, 7, 2 * BLK + 16, HDIM), bf16),
            pltpu.VMEM((2, 2, 2, BLK, HDIM), f32),
            pltpu.VMEM((2, NY, 2, 2, 32, HDIM), bf16),
            pltpu.VMEM((2, NY, 2, 2, 32, HDIM), bf16),
            pltpu.VMEM((2, NZ, 16, HDIM), f32),
            pltpu.VMEM((2, NZ, 16, HDIM), f32),
            pltpu.VMEM((2, NY, NZ, 16, HDIM), bf16),
        ]
        + [dma((2, NX))] * 4
        + [dma((2, 7))] * 2
        + [dma((2, NY))] * 2
        + [dma((2, NZ))] * 4
        + [dma((2, NY))] * 2
        + [dma((8,)), dma((5,))],
        compiler_params=pltpu.CompilerParams(
            collective_id=0, has_side_effects=True, vmem_limit_bytes=63 << 20
        ),
        name="attention_backward",
    )(branch_prefix, branch_blocks, queries, branch_keys, branch_values, grad_out, prefix_keys, prefix_values)
    return pl.pallas_call(
        hand_over,
        out_shape=out_shape,
        in_specs=[pl.BlockSpec(memory_space=pltpu.VMEM)] * 5,
        out_specs=[pl.BlockSpec(memory_space=pltpu.VMEM)] * 5,
        name="hand_over",
    )(*results)


def solution(mesh):
    split = P(("prefix", "branch"), None, "tensor")
    rows = P(None, "prefix", "tensor")
    ids = P(("prefix", "branch"))
    return jax.shard_map(
        body,
        mesh=mesh,
        in_specs=(split, split, split, split, rows, rows, ids, ids),
        out_specs=(split, split, split, rows, rows),
        check_vma=False,
    )
```

```python
import math

import jax
import jax.numpy as jnp
from jax import lax
from jax.experimental import pallas as pl
from jax.experimental.pallas import tpu as pltpu
from jax.sharding import PartitionSpec as P

HDIM = 128
BLK = 128
NX = 4
NY = 4
NZ = 8
OWNERS = 2 * NX
GROUP = 4
SCALE = 1.0 / math.sqrt(HDIM)
SCALE2 = SCALE * math.log2(math.e)
MESH = pl.DeviceIdType.MESH

STEPS = (2, 1, 3)
RELS = [(d, dc) for d in STEPS for dc in range(2)] + [(0, 1)]
ROWS = BLK // NY


def nt(a, b):
    return lax.dot_general(a, b, (((1,), (1,)), ((), ())), preferred_element_type=jnp.float32)


def tn(a, b):
    return lax.dot_general(a, b, (((0,), (0,)), ((), ())), preferred_element_type=jnp.float32)


def nn(a, b):
    return lax.dot_general(a, b, (((1,), (0,)), ((), ())), preferred_element_type=jnp.float32)


def fold(a, op):
    return op(a.reshape(a.shape[0] // 8, 8, a.shape[1]), axis=0)


def kernel(
    bp_ref,
    bb_ref,
    q_hbm,
    bk_hbm,
    bv_hbm,
    do_hbm,
    pk_hbm,
    pv_hbm,
    gq_hbm,
    gbk_hbm,
    gbv_hbm,
    gpk_hbm,
    gpv_hbm,
    q_ref,
    bk_ref,
    bv_ref,
    do_ref,
    gq_ref,
    gbk_ref,
    gbv_ref,
    gpk_ref,
    gpv_ref,
    kva,
    kvb,
    keys,
    qs,
    dos,
    s_buf,
    dp_buf,
    p_buf,
    ds_buf,
    own,
    term,
    got,
    acc,
    ys,
    yr,
    zs,
    zr,
    fin,
    a_s,
    a_r,
    b_s,
    b_r,
    u_s,
    u_r,
    ca_s,
    ca_r,
    cb_s,
    cb_r,
    t_s,
    t_r,
    y_s,
    y_r,
    z_s,
    z_r,
    za_s,
    za_r,
    ya_s,
    ya_r,
    in_s,
    out_s,
):
    me = lax.axis_index("prefix")
    b = lax.axis_index("branch")
    x, c = me // 2, lax.rem(me, 2)
    z, y = b // NY, lax.rem(b, NY)

    def at(dx=0, dc=0, dy=0, dz=0):
        return {
            "prefix": lax.rem(x + dx + NX, NX) * 2 + lax.rem(c + dc, 2),
            "branch": lax.rem(z + dz, NZ) * NY + lax.rem(y + dy + NY, NY),
        }

    def send(src, dst, ss, rs, dev):
        cp = pltpu.make_async_remote_copy(
            src_ref=src, dst_ref=dst, send_sem=ss, recv_sem=rs, device_id=dev, device_id_type=MESH
        )
        cp.start()
        return cp

    def local(src, dst, sem):
        cp = pltpu.make_async_copy(src, dst, sem)
        cp.start()
        return cp

    prefix_in = []
    for kind, ref in enumerate((pk_hbm, pv_hbm)):
        for r in range(NY):
            at_row = pl.multiple_of(lax.rem(y - r + NY, NY) * ROWS, ROWS)
            part = ref.at[:, pl.ds(at_row, ROWS), pl.ds(HDIM, HDIM)]
            prefix_in.append(local(part, kvb.at[0, 0, r, kind], in_s.at[NY * kind + r]))
        part = ref.at[:, :, pl.ds(0, HDIM)]
        prefix_in.append(local(part, kva.at[0, 0, kind], in_s.at[2 * NY + kind]))
    branch_in = [
        local(src, dst, in_s.at[2 * NY + 2 + i])
        for i, (src, dst) in enumerate(
            ((bk_hbm, bk_ref), (bv_hbm, bv_ref), (q_hbm, q_ref), (do_hbm, do_ref))
        )
    ]

    barrier = pltpu.get_barrier_semaphore()
    peers = [at(dx=-d, dc=dc) for d, dc in RELS] + [at(dy=-d, dc=dc) for d, dc in RELS[:-1]]
    peers += [at(dz=d) for d in range(1, NZ)]
    for dev in peers:
        pl.semaphore_signal(barrier, inc=1, device_id=dev, device_id_type=MESH)

    pid = bp_ref[0]
    for cp in prefix_in:
        cp.wait()
    pl.semaphore_wait(barrier, len(peers))

    rest = pl.ds(1, NX - 1)
    first_b = [
        send(kvb.at[0, 0, 0], kvb.at[0, d, 0], b_s.at[d], b_r.at[d], at(dx=d)) for d in range(1, NX)
    ]
    first_a = {
        d: send(kva.at[0, 0], kva.at[0, d], a_s.at[d], a_r.at[d], at(dx=d)) for d in (1, 3, 2)
    }
    over_a = {0: send(kva.at[0, 0], kva.at[1, 0], ca_s.at[0], ca_r.at[0], at(dc=1))}
    over_b = {NY: send(kvb.at[0, 0], kvb.at[1, 0], cb_s.at[NY], cb_r.at[NY], at(dc=1))}

    for cp in branch_in:
        cp.wait()
    live = lax.broadcasted_iota(jnp.int32, (BLK, HDIM), 0) < bb_ref[0] * BLK
    for g in range(2):
        for h in range(GROUP):
            wide = pl.ds((g * GROUP + h) * HDIM, HDIM)
            qs[g, pl.ds(h * BLK, BLK)] = q_ref[0, :, wide]
            grad = do_ref[0, :, wide]
            dos[g, pl.ds(h * BLK, BLK)] = jnp.where(live, grad, jnp.zeros_like(grad))

    def scores(g, slot, k, v, peak=None):
        s = nt(k, qs[g])
        if slot == OWNERS:
            key = lax.broadcasted_iota(jnp.int32, s.shape, 0)
            query = lax.rem(lax.broadcasted_iota(jnp.int32, s.shape, 1), BLK)
            s = jnp.where(key <= query, s, -1e30)
        s_buf[g, slot] = s
        dp_buf[g, slot] = nt(v, dos[g])
        top = fold(s, jnp.max)
        return top if peak is None else jnp.maximum(peak, top)

    def prefix_scores(g, other, d, peak):
        if g == 0:
            pairs = [[kva[other, d, kind, p] for p in range(2)] for kind in range(2)]
        else:
            pairs = [
                [kvb[other, d, :, kind, p].reshape(BLK, HDIM) for p in range(2)] for kind in range(2)
            ]
        k, v = [jnp.where(pid == 0, pair[0], pair[1]) for pair in pairs]
        slot = other * NX + d
        keys[g, slot] = k
        return scores(g, slot, k, v, peak)

    def own_columns(g):
        return pl.ds(g * HDIM, HDIM)

    peaks = []
    for g in range(2):
        cols = own_columns(g)
        peaks.append(scores(g, OWNERS, bk_ref[0, :, cols], bv_ref[0, :, cols]))
        peaks[g] = prefix_scores(g, 0, 0, peaks[g])
    for cp in first_b:
        cp.wait_recv()
    mine = kvb.at[0, rest, 0]
    second_b = {d: send(mine, kvb.at[0, rest, d], u_s.at[d], u_r.at[d], at(dy=d)) for d in (1, 3, 2)}
    over_b[0] = send(mine, kvb.at[1, rest, 0], cb_s.at[0], cb_r.at[0], at(dc=1))
    for d in (1, 3, 2):
        first_a[d].wait_recv()
        over_a[d] = send(kva.at[0, d], kva.at[1, d], ca_s.at[d], ca_r.at[d], at(dc=1))
        peaks[0] = prefix_scores(0, 0, d, peaks[0])
    for d in (1, 3, 2):
        second_b[d].wait_recv()
        here, there = kvb.at[0, rest, d], kvb.at[1, rest, d]
        over_b[d] = send(here, there, cb_s.at[d], cb_r.at[d], at(dc=1))
    for d in (0, 1, 3, 2):
        over_a[d].wait_recv()
        peaks[0] = prefix_scores(0, 1, d, peaks[0])
    sent = first_b + list(first_a.values()) + list(over_a.values())
    sent += list(second_b.values()) + list(over_b.values())

    width = GROUP * BLK
    terms = {}
    for g in range(2):
        cols = own_columns(g)
        if g == 1:
            for d in (1, 3, 2):
                peaks[1] = prefix_scores(1, 0, d, peaks[1])
            for d in (NY, 0, 1, 3, 2):
                over_b[d].wait_recv()
            for d in range(NX):
                peaks[1] = prefix_scores(1, 1, d, peaks[1])
        top = jnp.max(peaks[g], axis=0, keepdims=True) * SCALE2

        def exps(i, total):
            e = jnp.exp2(s_buf[g, i] * SCALE2 - top)
            s_buf[g, i] = e
            return total + fold(e, jnp.sum)

        total = lax.fori_loop(0, OWNERS + 1, exps, jnp.zeros((8, width), jnp.float32))
        share = 1.0 / jnp.sum(total, axis=0, keepdims=True)

        def probs(i, total):
            p = s_buf[g, i] * share
            low = p.astype(jnp.bfloat16)
            s_buf[g, i] = p
            p_buf[g, i] = low
            return total + fold(low.astype(jnp.float32) * dp_buf[g, i], jnp.sum)

        total = lax.fori_loop(0, OWNERS + 1, probs, jnp.zeros((8, width), jnp.float32))
        delta = jnp.sum(total, axis=0, keepdims=True)

        def grads(i):
            ds = (s_buf[g, i] * (dp_buf[g, i] - delta)).astype(jnp.bfloat16)
            ds_buf[g, i] = ds
            return nn(ds, qs[g]) * SCALE, nn(p_buf[g, i], dos[g])

        whose = jnp.full((16, HDIM), pid, jnp.int32).astype(jnp.float32).astype(jnp.bfloat16)
        for k, (d, dc) in enumerate(RELS):
            term[g, k, 2 * BLK : 2 * BLK + 16] = whose
        if g == 0:
            for k, (d, dc) in enumerate(RELS):
                for kind, part in enumerate(grads(dc * NX + d)):
                    term[0, k, kind * BLK : (kind + 1) * BLK] = part.astype(jnp.bfloat16)
                terms[0, k] = send(term.at[0, k], got.at[0, k], t_s.at[0, k], t_r.at[0, k], at(dx=-d, dc=dc))
            for kind, part in enumerate(grads(0)):
                own[0, kind * BLK : (kind + 1) * BLK] = part
        else:
            for dc in range(2):
                for d in range(NX):
                    for kind, part in enumerate(grads(dc * NX + d)):
                        low = part.astype(jnp.bfloat16)
                        at_row = (2 * d + kind) * ROWS
                        for k, (r, other) in enumerate(RELS):
                            if other == dc:
                                term[1, k, at_row : at_row + ROWS] = low[r * ROWS : (r + 1) * ROWS]
                        if dc == 0:
                            own[1, at_row : at_row + ROWS] = part[0:ROWS]
                for k, (r, other) in enumerate(RELS):
                    if other == dc:
                        terms[1, k] = send(
                            term.at[1, k], got.at[1, k], t_s.at[1, k], t_r.at[1, k], at(dy=-r, dc=dc)
                        )
        for ref, part in zip((gbk_ref, gbv_ref), grads(OWNERS)):
            ref[0, :, cols] = part.astype(jnp.bfloat16)
    for g in range(2):
        cols = own_columns(g)
        dq = tn(keys[g].reshape(OWNERS * BLK, HDIM), ds_buf[g, 0:OWNERS].reshape(OWNERS * BLK, width))
        dq = (dq + tn(bk_ref[0, :, cols], ds_buf[g, OWNERS])) * SCALE
        for h in range(GROUP):
            wide = pl.ds((g * GROUP + h) * HDIM, HDIM)
            gq_ref[0, :, wide] = dq[:, h * BLK : (h + 1) * BLK].T.astype(jnp.bfloat16)
    outs = [
        local(src, dst, out_s.at[i])
        for i, (src, dst) in enumerate(((gq_ref, gq_hbm), (gbk_ref, gbk_hbm), (gbv_ref, gbv_hbm)))
    ]
    sent += terms.values()

    second = {}
    for g in range(2):
        for k in range(len(RELS)):
            terms[g, k].wait_recv()
        for block in range(2 * NY):
            part = pl.ds(block * ROWS, ROWS)
            here = own[g, part]
            sums = [jnp.where(pid == p, here, 0.0) for p in range(2)]
            for k in range(len(RELS)):
                t = got[g, k, part].astype(jnp.float32)
                whose = got[g, k, 2 * BLK : 2 * BLK + 16].astype(jnp.float32)[0:1]
                first = jnp.broadcast_to(whose, t.shape) < 0.5
                sums[0] += jnp.where(first, t, 0.0)
                sums[1] += jnp.where(first, 0.0, t)
            kind, quarter = (block // NY, block % NY) if g == 0 else (block % 2, block // 2)
            for p in range(2):
                acc[g, quarter, p, kind] = sums[p]
                ys[g, quarter, p, kind] = sums[p].astype(jnp.bfloat16)
        for d in range(1, NY):
            src, dev = (lax.rem(y + d, NY), at(dy=d)) if g == 0 else (d, at(dx=-d))
            second[g, d] = send(ys.at[g, src], yr.at[g, d], y_s.at[g, d], y_r.at[g, d], dev)
    sent += second.values()

    along_z = {}
    for g in range(2):
        for d in range(1, NY):
            second[g, d].wait_recv()
        for p in range(2):
            for kind in range(2):
                total = acc[g, y if g == 0 else 0, p, kind]
                for d in range(1, NY):
                    total += yr[g, d, p, kind].astype(jnp.float32)
                zs[g, 4 * p + 2 * kind] = total[0:16]
                zs[g, 4 * p + 2 * kind + 1] = total[16:32]
        for d in range(1, NZ):
            src = zs.at[g, lax.rem(z + d, NZ)]
            along_z[g, d] = send(src, zr.at[g, d], z_s.at[g, d], z_r.at[g, d], at(dz=d))
    sent += along_z.values()

    back_z = {}
    for g in range(2):
        total = zs[g, z]
        for d in range(1, NZ):
            along_z[g, d].wait_recv()
            total += zr[g, d]
        fin[g, y, z] = total.astype(jnp.bfloat16)
        for d in range(1, NZ):
            here = fin.at[g, y, z]
            back_z[g, d] = send(here, here, za_s.at[g, d], za_r.at[g, d], at(dz=d))
    sent += back_z.values()

    back_y = {}
    for g in range(2):
        for d in range(1, NZ):
            back_z[g, d].wait_recv()
        for d in range(1, NY):
            here = fin.at[g, y]
            back_y[g, d] = send(here, here, ya_s.at[g, d], ya_r.at[g, d], at(dy=d))
    sent += back_y.values()

    for g in range(2):
        cols = own_columns(g)
        for d in range(1, NY):
            back_y[g, d].wait_recv()
        for quarter in range(NY):
            for p in range(2):
                for low in range(2):
                    row = pl.ds(quarter * ROWS + low * 16, 16)
                    gpk_ref[p, row, cols] = fin[g, quarter, 4 * p + low]
                    gpv_ref[p, row, cols] = fin[g, quarter, 4 * p + 2 + low]
    outs += [local(gpk_ref, gpk_hbm, out_s.at[3]), local(gpv_ref, gpv_hbm, out_s.at[4])]
    for cp in sent:
        cp.wait_send()
    for cp in outs:
        cp.wait()


def hand_over(*refs):
    for i in range(5):
        refs[5 + i][...] = refs[i][...]


def body(queries, branch_keys, branch_values, grad_out, prefix_keys, prefix_values, branch_prefix, branch_blocks):
    bf16, f32 = jnp.bfloat16, jnp.float32
    smem = pl.BlockSpec(memory_space=pltpu.SMEM)
    hbm = pl.BlockSpec(memory_space=pltpu.HBM)
    anywhere = pl.BlockSpec(memory_space=pl.ANY)
    width = GROUP * BLK
    dma = pltpu.SemaphoreType.DMA
    shapes = [a.shape for a in (queries, branch_keys, branch_values, prefix_keys, prefix_values)]
    wide, narrow, _, prefix, _ = (pltpu.VMEM(shape, bf16) for shape in shapes)
    out_shape = [jax.ShapeDtypeStruct(shape, bf16) for shape in shapes]
    results = pl.pallas_call(
        kernel,
        out_shape=out_shape,
        in_specs=[smem, smem] + [hbm] * 6,
        out_specs=[anywhere] * 5,
        scratch_shapes=[
            wide,
            narrow,
            narrow,
            wide,
            wide,
            narrow,
            narrow,
            prefix,
            prefix,
            pltpu.VMEM((2, NX, 2, 2, BLK, HDIM), bf16),
            pltpu.VMEM((2, NX, NY, 2, 2, ROWS, HDIM), bf16),
            pltpu.VMEM((2, OWNERS, BLK, HDIM), bf16),
            pltpu.VMEM((2, width, HDIM), bf16),
            pltpu.VMEM((2, width, HDIM), bf16),
            pltpu.VMEM((2, OWNERS + 1, BLK, width), f32),
            pltpu.VMEM((2, OWNERS + 1, BLK, width), f32),
            pltpu.VMEM((2, OWNERS + 1, BLK, width), bf16),
            pltpu.VMEM((2, OWNERS + 1, BLK, width), bf16),
            pltpu.VMEM((2, 2 * BLK, HDIM), f32),
            pltpu.VMEM((2, len(RELS), 2 * BLK + 16, HDIM), bf16),
            pltpu.VMEM((2, len(RELS), 2 * BLK + 16, HDIM), bf16),
            pltpu.VMEM((2, NY, 2, 2, ROWS, HDIM), f32),
            pltpu.VMEM((2, NY, 2, 2, ROWS, HDIM), bf16),
            pltpu.VMEM((2, NY, 2, 2, ROWS, HDIM), bf16),
            pltpu.VMEM((2, NZ, 16, HDIM), f32),
            pltpu.VMEM((2, NZ, 16, HDIM), f32),
            pltpu.VMEM((2, NY, NZ, 16, HDIM), bf16),
        ]
        + [dma((NX,))] * 4
        + [dma((NY,))] * 2
        + [dma((NX,))] * 2
        + [dma((NY + 1,))] * 2
        + [dma((2, len(RELS)))] * 2
        + [dma((2, NY))] * 2
        + [dma((2, NZ))] * 4
        + [dma((2, NY))] * 2
        + [dma((2 * NY + 6,)), dma((5,))],
        compiler_params=pltpu.CompilerParams(
            collective_id=0, has_side_effects=True, vmem_limit_bytes=63 << 20
        ),
        name="attention_backward",
    )(branch_prefix, branch_blocks, queries, branch_keys, branch_values, grad_out, prefix_keys, prefix_values)
    return pl.pallas_call(
        hand_over,
        out_shape=out_shape,
        in_specs=[pl.BlockSpec(memory_space=pltpu.VMEM)] * 5,
        out_specs=[pl.BlockSpec(memory_space=pltpu.VMEM)] * 5,
        name="hand_over",
    )(*results)


def solution(mesh):
    split = P(("prefix", "branch"), None, "tensor")
    rows = P(None, "prefix", "tensor")
    ids = P(("prefix", "branch"))
    return jax.shard_map(
        body,
        mesh=mesh,
        in_specs=(split, split, split, split, rows, rows, ids, ids),
        out_specs=(split, split, split, rows, rows),
        check_vma=False,
    )
```

```python
import math

import jax
import jax.numpy as jnp
from jax import lax
from jax.experimental import pallas as pl
from jax.experimental.pallas import tpu as pltpu
from jax.sharding import PartitionSpec as P

HDIM = 128
BLK = 128
NX = 4
NY = 4
NZ = 8
OWNERS = 2 * NX
GROUP = 4
SCALE = 1.0 / math.sqrt(HDIM)
SCALE2 = SCALE * math.log2(math.e)
MESH = pl.DeviceIdType.MESH

STEPS = (2, 1, 3)
RELS = [(d, dc) for d in STEPS for dc in range(2)] + [(0, 1)]
ROWS = BLK // NY


def nt(a, b):
    return lax.dot_general(a, b, (((1,), (1,)), ((), ())), preferred_element_type=jnp.float32)


def tn(a, b):
    return lax.dot_general(a, b, (((0,), (0,)), ((), ())), preferred_element_type=jnp.float32)


def nn(a, b):
    return lax.dot_general(a, b, (((1,), (0,)), ((), ())), preferred_element_type=jnp.float32)


def fold(a, op):
    return op(a.reshape(a.shape[0] // 8, 8, a.shape[1]), axis=0)


def kernel(
    bp_ref,
    bb_ref,
    q_hbm,
    bk_hbm,
    bv_hbm,
    do_hbm,
    pk_hbm,
    pv_hbm,
    gq_hbm,
    gbk_hbm,
    gbv_hbm,
    fin_hbm,
    q_ref,
    bk_ref,
    bv_ref,
    do_ref,
    gq_ref,
    gbk_ref,
    gbv_ref,
    kva,
    kvb,
    keys,
    qs,
    dos,
    s_buf,
    dp_buf,
    p_buf,
    ds_buf,
    dv_buf,
    own_k,
    own_v,
    term_k,
    term_v,
    got_k,
    got_v,
    acc,
    ys,
    yr,
    zs,
    zr,
    fin,
    a_s,
    a_r,
    b_s,
    b_r,
    u_s,
    u_r,
    ca_s,
    ca_r,
    cb_s,
    cb_r,
    tk_s,
    tk_r,
    tv_s,
    tv_r,
    y_s,
    y_r,
    z_s,
    z_r,
    za_s,
    za_r,
    ya_s,
    ya_r,
    in_s,
    out_s,
):
    me = lax.axis_index("prefix")
    b = lax.axis_index("branch")
    x, c = me // 2, lax.rem(me, 2)
    z, y = b // NY, lax.rem(b, NY)

    def at(dx=0, dc=0, dy=0, dz=0):
        return {
            "prefix": lax.rem(x + dx + NX, NX) * 2 + lax.rem(c + dc, 2),
            "branch": lax.rem(z + dz, NZ) * NY + lax.rem(y + dy + NY, NY),
        }

    def send(src, dst, ss, rs, dev):
        cp = pltpu.make_async_remote_copy(
            src_ref=src, dst_ref=dst, send_sem=ss, recv_sem=rs, device_id=dev, device_id_type=MESH
        )
        cp.start()
        return cp

    def local(src, dst, sem):
        cp = pltpu.make_async_copy(src, dst, sem)
        cp.start()
        return cp

    prefix_in = []
    for g in range(2):
        cols = pl.ds(g * HDIM, HDIM)
        for r in range(NY):
            at_row = pl.multiple_of(lax.rem(y - r + NY, NY) * ROWS, ROWS)
            part = pv_hbm.at[:, pl.ds(at_row, ROWS), cols]
            prefix_in.append(local(part, kvb.at[g, 0, 0, r], in_s.at[(NY + 1) * g + r]))
        prefix_in.append(local(pk_hbm.at[:, :, cols], kva.at[g, 0, 0], in_s.at[(NY + 1) * g + NY]))
    branch_in = [
        local(src, dst, in_s.at[2 * NY + 2 + i])
        for i, (src, dst) in enumerate(
            ((bk_hbm, bk_ref), (bv_hbm, bv_ref), (q_hbm, q_ref), (do_hbm, do_ref))
        )
    ]

    barrier = pltpu.get_barrier_semaphore()
    peers = [at(dx=-d, dc=dc) for d, dc in RELS] + [at(dy=-d, dc=dc) for d, dc in RELS[:-1]]
    peers += [at(dz=d) for d in range(1, NZ)]
    for dev in peers:
        pl.semaphore_signal(barrier, inc=1, device_id=dev, device_id_type=MESH)

    pid = bp_ref[0]
    for cp in prefix_in:
        cp.wait()
    pl.semaphore_wait(barrier, len(peers))

    rest = pl.ds(1, NX - 1)
    ones = range(1, NX)
    first_a, first_b, second_b, over_a, over_b = [], [], [], [], []

    def start_values(g):
        own_v = kvb.at[g, 0, 0, 0]
        first_b.append([send(own_v, kvb.at[g, 0, d, 0], b_s.at[g, d], b_r.at[g, d], at(dx=d)) for d in ones])

    def start_keys(g):
        own_k, own_v = kva.at[g, 0, 0], kvb.at[g, 0, 0]
        first_a.append([send(own_k, kva.at[g, 0, d], a_s.at[g, d], a_r.at[g, d], at(dx=d)) for d in ones])
        over_a.append([send(own_k, kva.at[g, 1, 0], ca_s.at[g, 0], ca_r.at[g, 0], at(dc=1))])
        over_b.append([send(own_v, kvb.at[g, 1, 0], cb_s.at[g, NY], cb_r.at[g, NY], at(dc=1))])

    def pass_keys(g, d):
        first_a[g][d - 1].wait_recv()
        over_a[g].append(send(kva.at[g, 0, d], kva.at[g, 1, d], ca_s.at[g, d], ca_r.at[g, d], at(dc=1)))

    def pass_values(g, d):
        if d:
            second_b[g][d - 1].wait_recv()
        here, there = kvb.at[g, 0, rest, d], kvb.at[g, 1, rest, d]
        over_b[g].append(send(here, there, cb_s.at[g, d], cb_r.at[g, d], at(dc=1)))

    def spread_values(g):
        for cp in first_b[g]:
            cp.wait_recv()
        here = kvb.at[g, 0, rest, 0]
        second_b.append([send(here, kvb.at[g, 0, rest, d], u_s.at[g, d], u_r.at[g, d], at(dy=d)) for d in ones])
        pass_values(g, 0)

    for g in range(2):
        start_values(g)
    for g in range(2):
        start_keys(g)

    for cp in branch_in:
        cp.wait()
    live = lax.broadcasted_iota(jnp.int32, (BLK, HDIM), 0) < bb_ref[0] * BLK
    for g in range(2):
        for h in range(GROUP):
            wide = pl.ds((g * GROUP + h) * HDIM, HDIM)
            qs[g, pl.ds(h * BLK, BLK)] = q_ref[0, :, wide]
            grad = do_ref[0, :, wide]
            dos[g, pl.ds(h * BLK, BLK)] = jnp.where(live, grad, jnp.zeros_like(grad))

    width = GROUP * BLK
    groups = [[], []]

    def own_columns(g):
        return pl.ds(g * HDIM, HDIM)

    def scores(g, slot, count, k, v):
        s = nt(k, qs[g]) * SCALE2
        if slot == OWNERS:
            key = lax.broadcasted_iota(jnp.int32, s.shape, 0)
            query = lax.rem(lax.broadcasted_iota(jnp.int32, s.shape, 1), BLK)
            s = jnp.where(key <= query, s, -1e30)
        s_buf[g, slot : slot + count] = s.reshape(count, BLK, width)
        dp_buf[g, slot : slot + count] = nt(v, dos[g]).reshape(count, BLK, width)
        top = jnp.max(fold(s, jnp.max), axis=0, keepdims=True)
        if groups[g]:
            top = jnp.maximum(top, groups[g][-1][2])

        def exps(i, total):
            e = jnp.exp2(s_buf[g, i] - top)
            s_buf[g, i] = e
            return total + fold(e, jnp.sum)

        total = lax.fori_loop(slot, slot + count, exps, jnp.zeros((8, width), jnp.float32))
        groups[g].append((slot, count, top, total))

    def prefix_scores(g, other, d, count):
        part = pl.ds(d, count)
        ks = [kva[g, other, part, p].reshape(count * BLK, HDIM) for p in range(2)]
        rows = [lax.rem(y - q + NY, NY) for q in range(NY)]
        vs = [
            jnp.concatenate([kvb[g, other, part, r, p][:, None] for r in rows], axis=1)
            .reshape(count * BLK, HDIM)
            for p in range(2)
        ]
        k, v = [jnp.where(pid == 0, pair[0], pair[1]) for pair in (ks, vs)]
        slot = other * NX + d
        keys[g, slot : slot + count] = k.reshape(count, BLK, HDIM)
        scores(g, slot, count, k, v)

    def first_scores(g):
        cols = own_columns(g)
        scores(g, OWNERS, 1, bk_ref[0, :, cols], bv_ref[0, :, cols])
        prefix_scores(g, 0, 0, 1)

    terms_k, terms_v = {}, {}

    def backward(g):
        cols = own_columns(g)
        top = groups[g][-1][2]
        scales = [jnp.exp2(m - top) for _, _, m, _ in groups[g]]
        share = 1.0 / sum(
            jnp.sum(part[3], axis=0, keepdims=True) * scale for part, scale in zip(groups[g], scales)
        )
        total = jnp.zeros((8, width), jnp.float32)
        for (slot, count, _, _), scale in zip(groups[g], scales):
            factor = scale * share

            def probs(i, running):
                low = (s_buf[g, i] * factor).astype(jnp.bfloat16)
                p_buf[g, i] = low
                return running + fold(low.astype(jnp.float32) * dp_buf[g, i], jnp.sum)

            total = lax.fori_loop(slot, slot + count, probs, total)
        delta = jnp.sum(total, axis=0, keepdims=True)
        whose = jnp.full((16, HDIM), pid, jnp.int32).astype(jnp.float32).astype(jnp.bfloat16)
        for k in range(len(RELS)):
            term_k[g, k, BLK : BLK + 16] = whose
            term_v[g, k, BLK : BLK + 16] = whose

        for dc in range(2):
            part = p_buf[g, dc * NX : (dc + 1) * NX].reshape(NX * BLK, width)
            dv_buf[dc] = nn(part, dos[g]).reshape(NX, NY, ROWS, HDIM)
            if dc == 0:
                own_v[g] = dv_buf[dc, :, y].reshape(BLK, HDIM)
            for k, (r, other) in enumerate(RELS):
                if other == dc:
                    there = dv_buf[dc, :, lax.rem(y - r + NY, NY)]
                    term_v[g, k, 0:BLK] = there.reshape(BLK, HDIM).astype(jnp.bfloat16)
                    terms_v[g, k] = send(
                        term_v.at[g, k], got_v.at[g, k], tv_s.at[g, k], tv_r.at[g, k], at(dy=-r, dc=dc)
                    )
        for (slot, count, _, _), scale in zip(groups[g], scales):
            factor = scale * share

            def slopes(i, _):
                p = s_buf[g, i] * factor
                ds_buf[g, i] = (p * (dp_buf[g, i] - delta)).astype(jnp.bfloat16)
                return 0

            lax.fori_loop(slot, slot + count, slopes, 0)
        for dc in range(2):
            part = ds_buf[g, dc * NX : (dc + 1) * NX].reshape(NX * BLK, width)
            dk = (nn(part, qs[g]) * SCALE).reshape(NX, BLK, HDIM)
            if dc == 0:
                own_k[g] = dk[0]
            for k, (d, other) in enumerate(RELS):
                if other == dc:
                    term_k[g, k, 0:BLK] = dk[d].astype(jnp.bfloat16)
                    terms_k[g, k] = send(
                        term_k.at[g, k], got_k.at[g, k], tk_s.at[g, k], tk_r.at[g, k], at(dx=-d, dc=dc)
                    )

    def queries_and_branch(g):
        cols = own_columns(g)
        gbk_ref[0, :, cols] = (nn(ds_buf[g, OWNERS], qs[g]) * SCALE).astype(jnp.bfloat16)
        gbv_ref[0, :, cols] = nn(p_buf[g, OWNERS], dos[g]).astype(jnp.bfloat16)
        dq = tn(keys[g].reshape(OWNERS * BLK, HDIM), ds_buf[g, 0:OWNERS].reshape(OWNERS * BLK, width))
        dq = (dq + tn(bk_ref[0, :, cols], ds_buf[g, OWNERS])) * SCALE
        for h in range(GROUP):
            wide = pl.ds((g * GROUP + h) * HDIM, HDIM)
            gq_ref[0, :, wide] = dq[:, h * BLK : (h + 1) * BLK].T.astype(jnp.bfloat16)

    first_scores(0)
    spread_values(0)
    spread_values(1)
    for d in (1, 3, 2):
        pass_keys(0, d)
    for d in (1, 3, 2):
        pass_values(0, d)
    prefix_scores(0, 0, 1, NX - 1)
    for cp in over_a[0] + over_b[0]:
        cp.wait_recv()
    prefix_scores(0, 1, 0, NX)
    backward(0)
    for d in (1, 3, 2):
        pass_keys(1, d)
    for d in (1, 3, 2):
        pass_values(1, d)
    first_scores(1)
    prefix_scores(1, 0, 1, NX - 1)
    for cp in over_a[1] + over_b[1]:
        cp.wait_recv()
    prefix_scores(1, 1, 0, NX)
    backward(1)
    for g in range(2):
        queries_and_branch(g)
    sent = sum(first_a + first_b + second_b + over_a + over_b, [])
    outs = [
        local(src, dst, out_s.at[i])
        for i, (src, dst) in enumerate(((gq_ref, gq_hbm), (gbk_ref, gbk_hbm), (gbv_ref, gbv_hbm)))
    ]
    sent += list(terms_k.values()) + list(terms_v.values())

    second = {}

    def first_sum(g, kind):
        terms, got, own = ((terms_k, got_k, own_k), (terms_v, got_v, own_v))[kind]
        for k in range(len(RELS)):
            terms[g, k].wait_recv()
        for quarter in range(NY):
            part = pl.ds(quarter * ROWS, ROWS)
            here = own[g, part]
            sums = [jnp.where(pid == p, here, 0.0) for p in range(2)]
            for k in range(len(RELS)):
                t = got[g, k, part].astype(jnp.float32)
                whose = got[g, k, BLK : BLK + 16].astype(jnp.float32)[0:1]
                first = jnp.broadcast_to(whose, t.shape) < 0.5
                sums[0] += jnp.where(first, t, 0.0)
                sums[1] += jnp.where(first, 0.0, t)
            for p in range(2):
                acc[g, kind, quarter, p] = sums[p]
                ys[g, kind, quarter, p] = sums[p].astype(jnp.bfloat16)
        for d in range(1, NY):
            src, dev = (lax.rem(y + d, NY), at(dy=d)) if kind == 0 else (d, at(dx=-d))
            here, there = ys.at[g, kind, src], yr.at[g, kind, d]
            second[g, kind, d] = send(here, there, y_s.at[g, kind, d], y_r.at[g, kind, d], dev)

    for g in range(2):
        first_sum(g, 1)
        first_sum(g, 0)
    sent += second.values()

    along_z = {}
    for g in range(2):
        for kind in (1, 0):
            for d in range(1, NY):
                second[g, kind, d].wait_recv()
            for p in range(2):
                total = acc[g, kind, y if kind == 0 else 0, p]
                for d in range(1, NY):
                    total += yr[g, kind, d, p].astype(jnp.float32)
                zs[g, 4 * p + 2 * kind] = total[0:16]
                zs[g, 4 * p + 2 * kind + 1] = total[16:32]
        for d in range(1, NZ):
            src = zs.at[g, lax.rem(z + d, NZ)]
            along_z[g, d] = send(src, zr.at[g, d], z_s.at[g, d], z_r.at[g, d], at(dz=d))
    sent += along_z.values()

    back_z = {}
    for g in range(2):
        total = zs[g, z]
        for d in range(1, NZ):
            along_z[g, d].wait_recv()
            total += zr[g, d]
        fin[g, y, z] = total.astype(jnp.bfloat16)
        for d in range(1, NZ):
            here = fin.at[g, y, z]
            back_z[g, d] = send(here, here, za_s.at[g, d], za_r.at[g, d], at(dz=d))
    sent += back_z.values()

    back_y = {}
    for g in range(2):
        for d in range(1, NZ):
            back_z[g, d].wait_recv()
        for d in range(1, NY):
            here = fin.at[g, y]
            back_y[g, d] = send(here, here, ya_s.at[g, d], ya_r.at[g, d], at(dy=d))
    sent += back_y.values()

    for cp in back_y.values():
        cp.wait_recv()
    outs.append(local(fin, fin_hbm, out_s.at[3]))
    for cp in sent:
        cp.wait_send()
    for cp in outs:
        cp.wait()


def hand_over(gq_in, gbk_in, gbv_in, fin, gq_ref, gbk_ref, gbv_ref, gpk_ref, gpv_ref):
    gq_ref[...] = gq_in[...]
    gbk_ref[...] = gbk_in[...]
    gbv_ref[...] = gbv_in[...]
    for g in range(2):
        cols = pl.ds(g * HDIM, HDIM)
        for quarter in range(NY):
            for p in range(2):
                for low in range(2):
                    row = pl.ds(quarter * ROWS + low * 16, 16)
                    gpk_ref[p, row, cols] = fin[g, quarter, 4 * p + low]
                    gpv_ref[p, row, cols] = fin[g, quarter, 4 * p + 2 + low]


def body(queries, branch_keys, branch_values, grad_out, prefix_keys, prefix_values, branch_prefix, branch_blocks):
    bf16, f32 = jnp.bfloat16, jnp.float32
    smem = pl.BlockSpec(memory_space=pltpu.SMEM)
    hbm = pl.BlockSpec(memory_space=pltpu.HBM)
    anywhere = pl.BlockSpec(memory_space=pl.ANY)
    width = GROUP * BLK
    dma = pltpu.SemaphoreType.DMA
    shapes = [a.shape for a in (queries, branch_keys, branch_values, prefix_keys, prefix_values)]
    wide, narrow = (pltpu.VMEM(shape, bf16) for shape in shapes[:2])
    out_shape = [jax.ShapeDtypeStruct(shape, bf16) for shape in shapes]
    results = pl.pallas_call(
        kernel,
        out_shape=out_shape[:3] + [jax.ShapeDtypeStruct((2, NY, NZ, 16, HDIM), bf16)],
        in_specs=[smem, smem] + [hbm] * 6,
        out_specs=[anywhere] * 4,
        scratch_shapes=[
            wide,
            narrow,
            narrow,
            wide,
            wide,
            narrow,
            narrow,
            pltpu.VMEM((2, 2, NX, 2, BLK, HDIM), bf16),
            pltpu.VMEM((2, 2, NX, NY, 2, ROWS, HDIM), bf16),
            pltpu.VMEM((2, OWNERS, BLK, HDIM), bf16),
            pltpu.VMEM((2, width, HDIM), bf16),
            pltpu.VMEM((2, width, HDIM), bf16),
            pltpu.VMEM((2, OWNERS + 1, BLK, width), f32),
            pltpu.VMEM((2, OWNERS + 1, BLK, width), f32),
            pltpu.VMEM((2, OWNERS + 1, BLK, width), bf16),
            pltpu.VMEM((2, OWNERS + 1, BLK, width), bf16),
            pltpu.VMEM((2, NX, NY, ROWS, HDIM), f32),
            pltpu.VMEM((2, BLK, HDIM), f32),
            pltpu.VMEM((2, BLK, HDIM), f32),
        ]
        + [pltpu.VMEM((2, len(RELS), BLK + 16, HDIM), bf16)] * 4
        + [
            pltpu.VMEM((2, 2, NY, 2, ROWS, HDIM), f32),
            pltpu.VMEM((2, 2, NY, 2, ROWS, HDIM), bf16),
            pltpu.VMEM((2, 2, NY, 2, ROWS, HDIM), bf16),
            pltpu.VMEM((2, NZ, 16, HDIM), f32),
            pltpu.VMEM((2, NZ, 16, HDIM), f32),
            pltpu.VMEM((2, NY, NZ, 16, HDIM), bf16),
        ]
        + [dma((2, NX))] * 8
        + [dma((2, NY + 1))] * 2
        + [dma((2, len(RELS)))] * 4
        + [dma((2, 2, NY))] * 2
        + [dma((2, NZ))] * 4
        + [dma((2, NY))] * 2
        + [dma((2 * NY + 6,)), dma((4,))],
        compiler_params=pltpu.CompilerParams(
            collective_id=0, has_side_effects=True, vmem_limit_bytes=63 << 20
        ),
        name="attention_backward",
    )(branch_prefix, branch_blocks, queries, branch_keys, branch_values, grad_out, prefix_keys, prefix_values)
    return pl.pallas_call(
        hand_over,
        out_shape=out_shape,
        in_specs=[pl.BlockSpec(memory_space=pltpu.VMEM)] * 4,
        out_specs=[pl.BlockSpec(memory_space=pltpu.VMEM)] * 5,
        name="hand_over",
    )(*results)


def solution(mesh):
    split = P(("prefix", "branch"), None, "tensor")
    rows = P(None, "prefix", "tensor")
    ids = P(("prefix", "branch"))
    return jax.shard_map(
        body,
        mesh=mesh,
        in_specs=(split, split, split, split, rows, rows, ids, ids),
        out_specs=(split, split, split, rows, rows),
        check_vma=False,
    )
```

```python
import math

import jax
import jax.numpy as jnp
from jax import lax
from jax.experimental import pallas as pl
from jax.experimental.pallas import tpu as pltpu
from jax.sharding import PartitionSpec as P

HDIM = 128
BLK = 128
NX = 4
NY = 4
NZ = 8
OWNERS = 2 * NX
GROUP = 4
SCALE = 1.0 / math.sqrt(HDIM)
SCALE2 = SCALE * math.log2(math.e)
MESH = pl.DeviceIdType.MESH

STEPS = (2, 1, 3)
RELS = [(d, dc) for d in STEPS for dc in range(2)] + [(0, 1)]
ROWS = BLK // NY


def nt(a, b):
    return lax.dot_general(a, b, (((1,), (1,)), ((), ())), preferred_element_type=jnp.float32)


def tn(a, b):
    return lax.dot_general(a, b, (((0,), (0,)), ((), ())), preferred_element_type=jnp.float32)


def nn(a, b):
    return lax.dot_general(a, b, (((1,), (0,)), ((), ())), preferred_element_type=jnp.float32)


def fold(a, op):
    return op(a.reshape(a.shape[0] // 8, 8, a.shape[1]), axis=0)


def kernel(
    bp_ref,
    bb_ref,
    q_hbm,
    bk_hbm,
    bv_hbm,
    do_hbm,
    pk_hbm,
    pv_hbm,
    gq_hbm,
    gbk_hbm,
    gbv_hbm,
    fin_hbm,
    q_ref,
    bk_ref,
    bv_ref,
    do_ref,
    gq_ref,
    gbk_ref,
    gbv_ref,
    kva,
    kvb,
    keys,
    qs,
    dos,
    s_buf,
    dp_buf,
    p_buf,
    ds_buf,
    dv_buf,
    own_k,
    own_v,
    term_k,
    term_v,
    got_k,
    got_v,
    acc,
    ys,
    yr,
    zs,
    zr,
    fin,
    a_s,
    a_r,
    b_s,
    b_r,
    u_s,
    u_r,
    ca_s,
    ca_r,
    cb_s,
    cb_r,
    tk_s,
    tk_r,
    tv_s,
    tv_r,
    y_s,
    y_r,
    z_s,
    z_r,
    za_s,
    za_r,
    ya_s,
    ya_r,
    in_s,
    out_s,
    greet,
):
    me = lax.axis_index("prefix")
    b = lax.axis_index("branch")
    x, c = me // 2, lax.rem(me, 2)
    z, y = b // NY, lax.rem(b, NY)

    def at(dx=0, dc=0, dy=0, dz=0):
        return {
            "prefix": lax.rem(x + dx + NX, NX) * 2 + lax.rem(c + dc, 2),
            "branch": lax.rem(z + dz, NZ) * NY + lax.rem(y + dy + NY, NY),
        }

    def send(src, dst, ss, rs, dev):
        cp = pltpu.make_async_remote_copy(
            src_ref=src, dst_ref=dst, send_sem=ss, recv_sem=rs, device_id=dev, device_id_type=MESH
        )
        cp.start()
        return cp

    def local(src, dst, sem):
        cp = pltpu.make_async_copy(src, dst, sem)
        cp.start()
        return cp

    prefix_in = []
    for g in range(2):
        cols = pl.ds(g * HDIM, HDIM)
        for r in range(NY):
            at_row = pl.multiple_of(lax.rem(y - r + NY, NY) * ROWS, ROWS)
            part = pv_hbm.at[:, pl.ds(at_row, ROWS), cols]
            prefix_in.append(local(part, kvb.at[g, 0, 0, r], in_s.at[(NY + 1) * g + r]))
        prefix_in.append(local(pk_hbm.at[:, :, cols], kva.at[g, 0, 0], in_s.at[(NY + 1) * g + NY]))
    branch_in = [
        local(src, dst, in_s.at[2 * NY + 2 + i])
        for i, (src, dst) in enumerate(
            ((bk_hbm, bk_ref), (bv_hbm, bv_ref), (q_hbm, q_ref), (do_hbm, do_ref))
        )
    ]

    barrier = pltpu.get_barrier_semaphore()
    peers = [at(dx=-d, dc=dc) for d, dc in RELS] + [at(dy=-d, dc=dc) for d, dc in RELS[:-1]]
    flips = [at(dz=step * (1 - 2 * lax.rem(z // step, 2)) + NZ) for step in (1, 2, 4)]
    peers += flips
    for dev in peers:
        pl.semaphore_signal(barrier, inc=1, device_id=dev, device_id_type=MESH)

    pid = bp_ref[0]
    for cp in prefix_in:
        cp.wait()
    pl.semaphore_wait(barrier, len(peers))

    rest = pl.ds(1, NX - 1)
    ones = range(1, NX)
    first_a, first_b, second_b, over_a, over_b = [], [], [], [], []

    def start_values(g):
        own_v = kvb.at[g, 0, 0, 0]
        first_b.append([send(own_v, kvb.at[g, 0, d, 0], b_s.at[g, d], b_r.at[g, d], at(dx=d)) for d in ones])

    def start_keys(g):
        own_k, own_v = kva.at[g, 0, 0], kvb.at[g, 0, 0]
        first_a.append([send(own_k, kva.at[g, 0, d], a_s.at[g, d], a_r.at[g, d], at(dx=d)) for d in ones])
        over_a.append([send(own_k, kva.at[g, 1, 0], ca_s.at[g, 0], ca_r.at[g, 0], at(dc=1))])
        over_b.append([send(own_v, kvb.at[g, 1, 0], cb_s.at[g, NY], cb_r.at[g, NY], at(dc=1))])

    def pass_keys(g, d):
        first_a[g][d - 1].wait_recv()
        over_a[g].append(send(kva.at[g, 0, d], kva.at[g, 1, d], ca_s.at[g, d], ca_r.at[g, d], at(dc=1)))

    def pass_values(g, d):
        if d:
            second_b[g][d - 1].wait_recv()
        here, there = kvb.at[g, 0, rest, d], kvb.at[g, 1, rest, d]
        over_b[g].append(send(here, there, cb_s.at[g, d], cb_r.at[g, d], at(dc=1)))

    def spread_values(g):
        for cp in first_b[g]:
            cp.wait_recv()
        here = kvb.at[g, 0, rest, 0]
        second_b.append([send(here, kvb.at[g, 0, rest, d], u_s.at[g, d], u_r.at[g, d], at(dy=d)) for d in ones])
        pass_values(g, 0)

    for g in range(2):
        start_values(g)
    for g in range(2):
        start_keys(g)

    for cp in branch_in:
        cp.wait()
    live = lax.broadcasted_iota(jnp.int32, (BLK, HDIM), 0) < bb_ref[0] * BLK
    for g in range(2):
        for h in range(GROUP):
            wide = pl.ds((g * GROUP + h) * HDIM, HDIM)
            qs[g, pl.ds(h * BLK, BLK)] = q_ref[0, :, wide]
            grad = do_ref[0, :, wide]
            dos[g, pl.ds(h * BLK, BLK)] = jnp.where(live, grad, jnp.zeros_like(grad))

    width = GROUP * BLK
    groups = [[], []]

    def own_columns(g):
        return pl.ds(g * HDIM, HDIM)

    def scores(g, slot, count, k, v):
        s = nt(k, qs[g]) * SCALE2
        if slot == OWNERS:
            key = lax.broadcasted_iota(jnp.int32, s.shape, 0)
            query = lax.rem(lax.broadcasted_iota(jnp.int32, s.shape, 1), BLK)
            s = jnp.where(key <= query, s, -1e30)
        s_buf[g, slot : slot + count] = s.reshape(count, BLK, width)
        dp_buf[g, slot : slot + count] = nt(v, dos[g]).reshape(count, BLK, width)
        top = jnp.max(fold(s, jnp.max), axis=0, keepdims=True)
        if groups[g]:
            top = jnp.maximum(top, groups[g][-1][2])

        def exps(i, total):
            e = jnp.exp2(s_buf[g, i] - top)
            s_buf[g, i] = e
            return total + fold(e, jnp.sum)

        total = lax.fori_loop(slot, slot + count, exps, jnp.zeros((8, width), jnp.float32))
        groups[g].append((slot, count, top, total))

    def prefix_scores(g, other, d, count):
        part = pl.ds(d, count)
        ks = [kva[g, other, part, p].reshape(count * BLK, HDIM) for p in range(2)]
        rows = [lax.rem(y - q + NY, NY) for q in range(NY)]
        vs = [
            jnp.concatenate([kvb[g, other, part, r, p][:, None] for r in rows], axis=1)
            .reshape(count * BLK, HDIM)
            for p in range(2)
        ]
        k, v = [jnp.where(pid == 0, pair[0], pair[1]) for pair in (ks, vs)]
        slot = other * NX + d
        keys[g, slot : slot + count] = k.reshape(count, BLK, HDIM)
        scores(g, slot, count, k, v)

    def first_scores(g):
        cols = own_columns(g)
        scores(g, OWNERS, 1, bk_ref[0, :, cols], bv_ref[0, :, cols])
        prefix_scores(g, 0, 0, 1)

    terms_k, terms_v = {}, {}

    def backward(g):
        cols = own_columns(g)
        top = groups[g][-1][2]
        scales = [jnp.exp2(m - top) for _, _, m, _ in groups[g]]
        share = 1.0 / sum(
            jnp.sum(part[3], axis=0, keepdims=True) * scale for part, scale in zip(groups[g], scales)
        )
        total = jnp.zeros((8, width), jnp.float32)
        for (slot, count, _, _), scale in zip(groups[g], scales):
            factor = scale * share

            def probs(i, running):
                low = (s_buf[g, i] * factor).astype(jnp.bfloat16)
                p_buf[g, i] = low
                return running + fold(low.astype(jnp.float32) * dp_buf[g, i], jnp.sum)

            total = lax.fori_loop(slot, slot + count, probs, total)
        delta = jnp.sum(total, axis=0, keepdims=True)
        whose = jnp.full((16, HDIM), pid, jnp.int32).astype(jnp.float32).astype(jnp.bfloat16)
        if g == 0:
            for k in range(len(RELS)):
                term_k[g, k, BLK : BLK + 16] = whose
                term_v[g, k, BLK : BLK + 16] = whose
        part_sent = pl.ds(0, BLK + 16 if g == 0 else BLK)

        for dc in range(2):
            part = p_buf[g, dc * NX : (dc + 1) * NX].reshape(NX * BLK, width)
            dv_buf[dc] = nn(part, dos[g]).reshape(NX, NY, ROWS, HDIM)
            if dc == 0:
                own_v[g] = dv_buf[dc, :, y].reshape(BLK, HDIM)
            for k, (r, other) in enumerate(RELS):
                if other == dc:
                    there = dv_buf[dc, :, lax.rem(y - r + NY, NY)]
                    term_v[g, k, 0:BLK] = there.reshape(BLK, HDIM).astype(jnp.bfloat16)
                    terms_v[g, k] = send(
                        term_v.at[g, k, part_sent], got_v.at[g, k, part_sent], tv_s.at[g, k], tv_r.at[g, k], at(dy=-r, dc=dc)
                    )
        for (slot, count, _, _), scale in zip(groups[g], scales):
            factor = scale * share

            def slopes(i, _):
                p = s_buf[g, i] * factor
                ds_buf[g, i] = (p * (dp_buf[g, i] - delta)).astype(jnp.bfloat16)
                return 0

            lax.fori_loop(slot, slot + count, slopes, 0)
        for dc in range(2):
            part = ds_buf[g, dc * NX : (dc + 1) * NX].reshape(NX * BLK, width)
            dk = (nn(part, qs[g]) * SCALE).reshape(NX, BLK, HDIM)
            if dc == 0:
                own_k[g] = dk[0]
            for k, (d, other) in enumerate(RELS):
                if other == dc:
                    term_k[g, k, 0:BLK] = dk[d].astype(jnp.bfloat16)
                    terms_k[g, k] = send(
                        term_k.at[g, k, part_sent], got_k.at[g, k, part_sent], tk_s.at[g, k], tk_r.at[g, k], at(dx=-d, dc=dc)
                    )

    def queries_and_branch(g):
        cols = own_columns(g)
        gbk_ref[0, :, cols] = (nn(ds_buf[g, OWNERS], qs[g]) * SCALE).astype(jnp.bfloat16)
        gbv_ref[0, :, cols] = nn(p_buf[g, OWNERS], dos[g]).astype(jnp.bfloat16)
        dq = tn(keys[g].reshape(OWNERS * BLK, HDIM), ds_buf[g, 0:OWNERS].reshape(OWNERS * BLK, width))
        dq = (dq + tn(bk_ref[0, :, cols], ds_buf[g, OWNERS])) * SCALE
        for h in range(GROUP):
            wide = pl.ds((g * GROUP + h) * HDIM, HDIM)
            gq_ref[0, :, wide] = dq[:, h * BLK : (h + 1) * BLK].T.astype(jnp.bfloat16)

    for i in range(2):
        pl.semaphore_signal(greet.at[i], inc=1, device_id=flips[i], device_id_type=MESH)
        if i == 0:
            first_scores(0)
            spread_values(0)
            pl.semaphore_wait(greet.at[0], 1)
    spread_values(1)
    for d in (1, 3, 2):
        pass_keys(0, d)
    for d in (1, 3, 2):
        pass_values(0, d)
    prefix_scores(0, 0, 1, NX - 1)
    for cp in over_a[0] + over_b[0]:
        cp.wait_recv()
    prefix_scores(0, 1, 0, NX)
    backward(0)
    for d in (1, 3, 2):
        pass_keys(1, d)
    for d in (1, 3, 2):
        pass_values(1, d)
    first_scores(1)
    prefix_scores(1, 0, 1, NX - 1)
    for cp in over_a[1] + over_b[1]:
        cp.wait_recv()
    prefix_scores(1, 1, 0, NX)
    backward(1)
    for g in range(2):
        queries_and_branch(g)
    outs = [
        local(src, dst, out_s.at[i])
        for i, (src, dst) in enumerate(((gq_ref, gq_hbm), (gbk_ref, gbk_hbm), (gbv_ref, gbv_hbm)))
    ]
    for cp in sum(first_a + first_b + second_b + over_a + over_b, []):
        cp.wait_send()

    second = {}

    def first_sum(g, kind):
        terms, got, own = ((terms_k, got_k, own_k), (terms_v, got_v, own_v))[kind]
        for k in range(len(RELS)):
            terms[g, k].wait_recv()
        for quarter in range(NY):
            part = pl.ds(quarter * ROWS, ROWS)
            here = own[g, part]
            sums = [jnp.where(pid == p, here, 0.0) for p in range(2)]
            for k in range(len(RELS)):
                t = got[g, k, part].astype(jnp.float32)
                whose = got[0, k, BLK : BLK + 16].astype(jnp.float32)[0:1]
                first = jnp.broadcast_to(whose, t.shape) < 0.5
                sums[0] += jnp.where(first, t, 0.0)
                sums[1] += jnp.where(first, 0.0, t)
            for p in range(2):
                acc[g, kind, quarter, p] = sums[p]
                ys[g, kind, quarter, p] = sums[p].astype(jnp.bfloat16)
        for d in range(1, NY):
            src, dev = (lax.rem(y + d, NY), at(dy=d)) if kind == 0 else (d, at(dx=-d))
            here, there = ys.at[g, kind, src], yr.at[g, kind, d]
            second[g, kind, d] = send(here, there, y_s.at[g, kind, d], y_r.at[g, kind, d], dev)

    for g in range(2):
        first_sum(g, 1)
        first_sum(g, 0)
    for cp in list(terms_k.values()) + list(terms_v.values()):
        cp.wait_send()

    pl.semaphore_wait(greet.at[1], 1)
    along_z = {}
    for g in range(2):
        for kind in (1, 0):
            for d in range(1, NY):
                second[g, kind, d].wait_recv()
            for p in range(2):
                total = acc[g, kind, y if kind == 0 else 0, p]
                for d in range(1, NY):
                    total += yr[g, kind, d, p].astype(jnp.float32)
                zs[g, 4 * p + 2 * kind] = total[0:16]
                zs[g, 4 * p + 2 * kind + 1] = total[16:32]
        for d in range(1, NZ):
            src = zs.at[g, lax.rem(z + d, NZ)]
            along_z[g, d] = send(src, zr.at[g, d], z_s.at[g, d], z_r.at[g, d], at(dz=d))
    for cp in second.values():
        cp.wait_send()

    for g in range(2):
        total = zs[g, z]
        for d in range(1, NZ):
            along_z[g, d].wait_recv()
            total += zr[g, d]
        fin[y, z, g] = total.astype(jnp.bfloat16)
    here = fin.at[y, z]
    back_z = [send(here, here, za_s.at[d], za_r.at[d], at(dz=d)) for d in range(1, NZ)]
    for cp in along_z.values():
        cp.wait_send()
    for cp in outs:
        cp.wait()
    for cp in back_z:
        cp.wait_recv()
    here = fin.at[y]
    back_y = [send(here, here, ya_s.at[d], ya_r.at[d], at(dy=d)) for d in range(1, NY)]
    for cp in back_z:
        cp.wait_send()
    for cp in back_y:
        cp.wait_recv()
    last = local(fin, fin_hbm, out_s.at[3])
    for cp in back_y:
        cp.wait_send()
    last.wait()


def hand_over(gq_in, gbk_in, gbv_in, fin, gq_ref, gbk_ref, gbv_ref, gpk_ref, gpv_ref):
    gq_ref[...] = gq_in[...]
    gbk_ref[...] = gbk_in[...]
    gbv_ref[...] = gbv_in[...]
    for g in range(2):
        cols = pl.ds(g * HDIM, HDIM)
        for quarter in range(NY):
            for p in range(2):
                for low in range(2):
                    row = pl.ds(quarter * ROWS + low * 16, 16)
                    gpk_ref[p, row, cols] = fin[quarter, 4 * p + low, g]
                    gpv_ref[p, row, cols] = fin[quarter, 4 * p + 2 + low, g]


def body(queries, branch_keys, branch_values, grad_out, prefix_keys, prefix_values, branch_prefix, branch_blocks):
    bf16, f32 = jnp.bfloat16, jnp.float32
    smem = pl.BlockSpec(memory_space=pltpu.SMEM)
    hbm = pl.BlockSpec(memory_space=pltpu.HBM)
    anywhere = pl.BlockSpec(memory_space=pl.ANY)
    width = GROUP * BLK
    dma = pltpu.SemaphoreType.DMA
    shapes = [a.shape for a in (queries, branch_keys, branch_values, prefix_keys, prefix_values)]
    wide, narrow = (pltpu.VMEM(shape, bf16) for shape in shapes[:2])
    out_shape = [jax.ShapeDtypeStruct(shape, bf16) for shape in shapes]
    results = pl.pallas_call(
        kernel,
        out_shape=out_shape[:3] + [jax.ShapeDtypeStruct((NY, NZ, 2, 16, HDIM), bf16)],
        in_specs=[smem, smem] + [hbm] * 6,
        out_specs=[anywhere] * 4,
        scratch_shapes=[
            wide,
            narrow,
            narrow,
            wide,
            wide,
            narrow,
            narrow,
            pltpu.VMEM((2, 2, NX, 2, BLK, HDIM), bf16),
            pltpu.VMEM((2, 2, NX, NY, 2, ROWS, HDIM), bf16),
            pltpu.VMEM((2, OWNERS, BLK, HDIM), bf16),
            pltpu.VMEM((2, width, HDIM), bf16),
            pltpu.VMEM((2, width, HDIM), bf16),
            pltpu.VMEM((2, OWNERS + 1, BLK, width), f32),
            pltpu.VMEM((2, OWNERS + 1, BLK, width), f32),
            pltpu.VMEM((2, OWNERS + 1, BLK, width), bf16),
            pltpu.VMEM((2, OWNERS + 1, BLK, width), bf16),
            pltpu.VMEM((2, NX, NY, ROWS, HDIM), f32),
            pltpu.VMEM((2, BLK, HDIM), f32),
            pltpu.VMEM((2, BLK, HDIM), f32),
        ]
        + [pltpu.VMEM((2, len(RELS), BLK + 16, HDIM), bf16)] * 4
        + [
            pltpu.VMEM((2, 2, NY, 2, ROWS, HDIM), f32),
            pltpu.VMEM((2, 2, NY, 2, ROWS, HDIM), bf16),
            pltpu.VMEM((2, 2, NY, 2, ROWS, HDIM), bf16),
            pltpu.VMEM((2, NZ, 16, HDIM), f32),
            pltpu.VMEM((2, NZ, 16, HDIM), f32),
            pltpu.VMEM((NY, NZ, 2, 16, HDIM), bf16),
        ]
        + [dma((2, NX))] * 8
        + [dma((2, NY + 1))] * 2
        + [dma((2, len(RELS)))] * 4
        + [dma((2, 2, NY))] * 2
        + [dma((2, NZ))] * 2
        + [dma((NZ,))] * 2
        + [dma((NY,))] * 2
        + [dma((2 * NY + 6,)), dma((4,)), pltpu.SemaphoreType.REGULAR((2,))],
        compiler_params=pltpu.CompilerParams(
            collective_id=0, has_side_effects=True, vmem_limit_bytes=63 << 20
        ),
        name="attention_backward",
    )(branch_prefix, branch_blocks, queries, branch_keys, branch_values, grad_out, prefix_keys, prefix_values)
    return pl.pallas_call(
        hand_over,
        out_shape=out_shape,
        in_specs=[pl.BlockSpec(memory_space=pltpu.VMEM)] * 4,
        out_specs=[pl.BlockSpec(memory_space=pltpu.VMEM)] * 5,
        name="hand_over",
    )(*results)


def solution(mesh):
    split = P(("prefix", "branch"), None, "tensor")
    rows = P(None, "prefix", "tensor")
    ids = P(("prefix", "branch"))
    return jax.shard_map(
        body,
        mesh=mesh,
        in_specs=(split, split, split, split, rows, rows, ids, ids),
        out_specs=(split, split, split, rows, rows),
        check_vma=False,
    )
```

```python
import math

import jax
import jax.numpy as jnp
from jax import lax
from jax.experimental import pallas as pl
from jax.experimental.pallas import tpu as pltpu
from jax.sharding import PartitionSpec as P

HDIM = 128
BLK = 128
NX = 4
NY = 4
NZ = 8
OWNERS = 2 * NX
GROUP = 4
SCALE = 1.0 / math.sqrt(HDIM)
SCALE2 = SCALE * math.log2(math.e)
MESH = pl.DeviceIdType.MESH

STEPS = (2, 1, 3)
RELS = [(d, dc) for d in STEPS for dc in range(2)] + [(0, 1)]
ROWS = BLK // NY


def nt(a, b):
    return lax.dot_general(a, b, (((1,), (1,)), ((), ())), preferred_element_type=jnp.float32)


def tn(a, b):
    return lax.dot_general(a, b, (((0,), (0,)), ((), ())), preferred_element_type=jnp.float32)


def nn(a, b):
    return lax.dot_general(a, b, (((1,), (0,)), ((), ())), preferred_element_type=jnp.float32)


def fold(a, op):
    return op(a.reshape(a.shape[0] // 8, 8, a.shape[1]), axis=0)


def kernel(
    bp_ref,
    bb_ref,
    q_hbm,
    bk_hbm,
    bv_hbm,
    do_hbm,
    pk_hbm,
    pv_hbm,
    gq_hbm,
    gbk_hbm,
    gbv_hbm,
    fin_hbm,
    q_ref,
    bk_ref,
    bv_ref,
    do_ref,
    gq_ref,
    gbk_ref,
    gbv_ref,
    kva,
    kvb,
    keys,
    qs,
    dos,
    s_buf,
    dp_buf,
    p_buf,
    ds_buf,
    dv_buf,
    own_k,
    own_v,
    term_k,
    term_v,
    got_k,
    got_v,
    acc,
    ys,
    yr,
    zs,
    zr,
    fin,
    a_s,
    a_r,
    b_s,
    b_r,
    u_s,
    u_r,
    ca_s,
    ca_r,
    cb_s,
    cb_r,
    tk_s,
    tk_r,
    tv_s,
    tv_r,
    y_s,
    y_r,
    z_s,
    z_r,
    za_s,
    za_r,
    ya_s,
    ya_r,
    in_s,
    out_s,
    greet,
):
    me = lax.axis_index("prefix")
    b = lax.axis_index("branch")
    x, c = me // 2, lax.rem(me, 2)
    z, y = b // NY, lax.rem(b, NY)

    def at(dx=0, dc=0, dy=0, dz=0):
        return {
            "prefix": lax.rem(x + dx + NX, NX) * 2 + lax.rem(c + dc, 2),
            "branch": lax.rem(z + dz, NZ) * NY + lax.rem(y + dy + NY, NY),
        }

    def send(src, dst, ss, rs, dev):
        cp = pltpu.make_async_remote_copy(
            src_ref=src, dst_ref=dst, send_sem=ss, recv_sem=rs, device_id=dev, device_id_type=MESH
        )
        cp.start()
        return cp

    def local(src, dst, sem):
        cp = pltpu.make_async_copy(src, dst, sem)
        cp.start()
        return cp

    prefix_in = []
    for g in range(2):
        cols = pl.ds(g * HDIM, HDIM)
        for r in range(NY):
            at_row = pl.multiple_of(lax.rem(y - r + NY, NY) * ROWS, ROWS)
            part = pv_hbm.at[:, pl.ds(at_row, ROWS), cols]
            prefix_in.append(local(part, kvb.at[g, 0, 0, r], in_s.at[(NY + 1) * g + r]))
        prefix_in.append(local(pk_hbm.at[:, :, cols], kva.at[g, 0, 0], in_s.at[(NY + 1) * g + NY]))
    branch_in = [
        local(src, dst, in_s.at[2 * NY + 2 + i])
        for i, (src, dst) in enumerate(
            ((bk_hbm, bk_ref), (bv_hbm, bv_ref), (q_hbm, q_ref), (do_hbm, do_ref))
        )
    ]

    barrier = pltpu.get_barrier_semaphore()
    peers = [at(dx=-d, dc=dc) for d, dc in RELS] + [at(dy=-d, dc=dc) for d, dc in RELS[:-1]]
    flips = [at(dz=step * (1 - 2 * lax.rem(z // step, 2)) + NZ) for step in (1, 2, 4)]
    peers += flips
    for dev in peers:
        pl.semaphore_signal(barrier, inc=1, device_id=dev, device_id_type=MESH)

    pid = bp_ref[0]
    pl.semaphore_wait(barrier, len(peers))

    rest = pl.ds(1, NX - 1)
    ones = range(1, NX)
    first_a, first_b, second_b, over_a, over_b = [], [], [], [], []

    def start_values(g):
        own_v = pv_hbm.at[:, pl.ds(pl.multiple_of(y * ROWS, ROWS), ROWS), pl.ds(g * HDIM, HDIM)]
        first_b.append([send(own_v, kvb.at[g, 0, d, 0], b_s.at[g, d], b_r.at[g, d], at(dx=d)) for d in ones])

    def start_keys(g):
        own_k = pk_hbm.at[:, :, pl.ds(g * HDIM, HDIM)]
        first_a.append([send(own_k, kva.at[g, 0, d], a_s.at[g, d], a_r.at[g, d], at(dx=d)) for d in ones])

    def start_over(g):
        own_k, own_v = kva.at[g, 0, 0], kvb.at[g, 0, 0]
        over_a.append([send(own_k, kva.at[g, 1, 0], ca_s.at[g, 0], ca_r.at[g, 0], at(dc=1))])
        over_b.append([send(own_v, kvb.at[g, 1, 0], cb_s.at[g, NY], cb_r.at[g, NY], at(dc=1))])

    def pass_keys(g, d):
        first_a[g][d - 1].wait_recv()
        over_a[g].append(send(kva.at[g, 0, d], kva.at[g, 1, d], ca_s.at[g, d], ca_r.at[g, d], at(dc=1)))

    def pass_values(g, d):
        if d:
            second_b[g][d - 1].wait_recv()
        here, there = kvb.at[g, 0, rest, d], kvb.at[g, 1, rest, d]
        over_b[g].append(send(here, there, cb_s.at[g, d], cb_r.at[g, d], at(dc=1)))

    def spread_values(g):
        for cp in first_b[g]:
            cp.wait_recv()
        here = kvb.at[g, 0, rest, 0]
        second_b.append([send(here, kvb.at[g, 0, rest, d], u_s.at[g, d], u_r.at[g, d], at(dy=d)) for d in ones])
        pass_values(g, 0)

    for g in range(2):
        start_values(g)
    for g in range(2):
        start_keys(g)
    for cp in prefix_in:
        cp.wait()
    for g in range(2):
        start_over(g)

    for cp in branch_in:
        cp.wait()
    live = lax.broadcasted_iota(jnp.int32, (BLK, HDIM), 0) < bb_ref[0] * BLK
    for g in range(2):
        for h in range(GROUP):
            wide = pl.ds((g * GROUP + h) * HDIM, HDIM)
            qs[g, pl.ds(h * BLK, BLK)] = q_ref[0, :, wide]
            grad = do_ref[0, :, wide]
            dos[g, pl.ds(h * BLK, BLK)] = jnp.where(live, grad, jnp.zeros_like(grad))

    width = GROUP * BLK
    groups = [[], []]

    def own_columns(g):
        return pl.ds(g * HDIM, HDIM)

    def scores(g, slot, count, k, v):
        s = nt(k, qs[g]) * SCALE2
        if slot == OWNERS:
            key = lax.broadcasted_iota(jnp.int32, s.shape, 0)
            query = lax.rem(lax.broadcasted_iota(jnp.int32, s.shape, 1), BLK)
            s = jnp.where(key <= query, s, -1e30)
        s_buf[g, slot : slot + count] = s.reshape(count, BLK, width)
        dp_buf[g, slot : slot + count] = nt(v, dos[g]).reshape(count, BLK, width)
        top = jnp.max(fold(s, jnp.max), axis=0, keepdims=True)
        if groups[g]:
            top = jnp.maximum(top, groups[g][-1][2])

        def exps(i, total):
            e = jnp.exp2(s_buf[g, i] - top)
            s_buf[g, i] = e
            return total + fold(e, jnp.sum)

        total = lax.fori_loop(slot, slot + count, exps, jnp.zeros((8, width), jnp.float32))
        groups[g].append((slot, count, top, total))

    def prefix_scores(g, other, d, count):
        part = pl.ds(d, count)
        ks = [kva[g, other, part, p].reshape(count * BLK, HDIM) for p in range(2)]
        rows = [lax.rem(y - q + NY, NY) for q in range(NY)]
        vs = [
            jnp.concatenate([kvb[g, other, part, r, p][:, None] for r in rows], axis=1)
            .reshape(count * BLK, HDIM)
            for p in range(2)
        ]
        k, v = [jnp.where(pid == 0, pair[0], pair[1]) for pair in (ks, vs)]
        slot = other * NX + d
        keys[g, slot : slot + count] = k.reshape(count, BLK, HDIM)
        scores(g, slot, count, k, v)

    def first_scores(g):
        cols = own_columns(g)
        scores(g, OWNERS, 1, bk_ref[0, :, cols], bv_ref[0, :, cols])
        prefix_scores(g, 0, 0, 1)

    terms_k, terms_v = {}, {}

    def backward(g):
        cols = own_columns(g)
        top = groups[g][-1][2]
        scales = [jnp.exp2(m - top) for _, _, m, _ in groups[g]]
        share = 1.0 / sum(
            jnp.sum(part[3], axis=0, keepdims=True) * scale for part, scale in zip(groups[g], scales)
        )
        total = jnp.zeros((8, width), jnp.float32)
        for (slot, count, _, _), scale in zip(groups[g], scales):
            factor = scale * share

            def probs(i, running):
                low = (s_buf[g, i] * factor).astype(jnp.bfloat16)
                p_buf[g, i] = low
                return running + fold(low.astype(jnp.float32) * dp_buf[g, i], jnp.sum)

            total = lax.fori_loop(slot, slot + count, probs, total)
        delta = jnp.sum(total, axis=0, keepdims=True)
        whose = jnp.full((16, HDIM), pid, jnp.int32).astype(jnp.float32).astype(jnp.bfloat16)
        if g == 0:
            for k in range(len(RELS)):
                term_k[g, k, BLK : BLK + 16] = whose
                term_v[g, k, BLK : BLK + 16] = whose
        part_sent = pl.ds(0, BLK + 16 if g == 0 else BLK)

        for dc in range(2):
            part = p_buf[g, dc * NX : (dc + 1) * NX].reshape(NX * BLK, width)
            dv_buf[dc] = nn(part, dos[g]).reshape(NX, NY, ROWS, HDIM)
            if dc == 0:
                own_v[g] = dv_buf[dc, :, y].reshape(BLK, HDIM)
            for k, (r, other) in enumerate(RELS):
                if other == dc:
                    there = dv_buf[dc, :, lax.rem(y - r + NY, NY)]
                    term_v[g, k, 0:BLK] = there.reshape(BLK, HDIM).astype(jnp.bfloat16)
                    terms_v[g, k] = send(
                        term_v.at[g, k, part_sent], got_v.at[g, k, part_sent], tv_s.at[g, k], tv_r.at[g, k], at(dy=-r, dc=dc)
                    )
        for (slot, count, _, _), scale in zip(groups[g], scales):
            factor = scale * share

            def slopes(i, _):
                p = s_buf[g, i] * factor
                ds_buf[g, i] = (p * (dp_buf[g, i] - delta)).astype(jnp.bfloat16)
                return 0

            lax.fori_loop(slot, slot + count, slopes, 0)
        for dc in range(2):
            part = ds_buf[g, dc * NX : (dc + 1) * NX].reshape(NX * BLK, width)
            dk = (nn(part, qs[g]) * SCALE).reshape(NX, BLK, HDIM)
            if dc == 0:
                own_k[g] = dk[0]
            for k, (d, other) in enumerate(RELS):
                if other == dc:
                    term_k[g, k, 0:BLK] = dk[d].astype(jnp.bfloat16)
                    terms_k[g, k] = send(
                        term_k.at[g, k, part_sent], got_k.at[g, k, part_sent], tk_s.at[g, k], tk_r.at[g, k], at(dx=-d, dc=dc)
                    )

    def queries_and_branch(g):
        cols = own_columns(g)
        gbk_ref[0, :, cols] = (nn(ds_buf[g, OWNERS], qs[g]) * SCALE).astype(jnp.bfloat16)
        gbv_ref[0, :, cols] = nn(p_buf[g, OWNERS], dos[g]).astype(jnp.bfloat16)
        dq = tn(keys[g].reshape(OWNERS * BLK, HDIM), ds_buf[g, 0:OWNERS].reshape(OWNERS * BLK, width))
        dq = (dq + tn(bk_ref[0, :, cols], ds_buf[g, OWNERS])) * SCALE
        for h in range(GROUP):
            wide = pl.ds((g * GROUP + h) * HDIM, HDIM)
            gq_ref[0, :, wide] = dq[:, h * BLK : (h + 1) * BLK].T.astype(jnp.bfloat16)

    for i in range(2):
        pl.semaphore_signal(greet.at[i], inc=1, device_id=flips[i], device_id_type=MESH)
        if i == 0:
            first_scores(0)
            spread_values(0)
            pl.semaphore_wait(greet.at[0], 1)
    spread_values(1)
    for d in (1, 3, 2):
        pass_keys(0, d)
    for d in (1, 3, 2):
        pass_values(0, d)
    prefix_scores(0, 0, 1, NX - 1)
    for cp in over_a[0] + over_b[0]:
        cp.wait_recv()
    prefix_scores(0, 1, 0, NX)
    backward(0)
    for d in (1, 3, 2):
        pass_keys(1, d)
    for d in (1, 3, 2):
        pass_values(1, d)
    first_scores(1)
    prefix_scores(1, 0, 1, NX - 1)
    for cp in over_a[1] + over_b[1]:
        cp.wait_recv()
    prefix_scores(1, 1, 0, NX)
    backward(1)
    for g in range(2):
        queries_and_branch(g)
    outs = [
        local(src, dst, out_s.at[i])
        for i, (src, dst) in enumerate(((gq_ref, gq_hbm), (gbk_ref, gbk_hbm), (gbv_ref, gbv_hbm)))
    ]
    for cp in sum(first_a + first_b + second_b + over_a + over_b, []):
        cp.wait_send()

    second = {}

    def first_sum(g, kind):
        terms, got, own = ((terms_k, got_k, own_k), (terms_v, got_v, own_v))[kind]
        for k in range(len(RELS)):
            terms[g, k].wait_recv()
        for quarter in range(NY):
            part = pl.ds(quarter * ROWS, ROWS)
            here = own[g, part]
            sums = [jnp.where(pid == p, here, 0.0) for p in range(2)]
            for k in range(len(RELS)):
                t = got[g, k, part].astype(jnp.float32)
                whose = got[0, k, BLK : BLK + 16].astype(jnp.float32)[0:1]
                first = jnp.broadcast_to(whose, t.shape) < 0.5
                sums[0] += jnp.where(first, t, 0.0)
                sums[1] += jnp.where(first, 0.0, t)
            for p in range(2):
                acc[g, kind, quarter, p] = sums[p]
                ys[g, kind, quarter, p] = sums[p].astype(jnp.bfloat16)
        for d in range(1, NY):
            src, dev = (lax.rem(y + d, NY), at(dy=d)) if kind == 0 else (d, at(dx=-d))
            here, there = ys.at[g, kind, src], yr.at[g, kind, d]
            second[g, kind, d] = send(here, there, y_s.at[g, kind, d], y_r.at[g, kind, d], dev)

    for g in range(2):
        first_sum(g, 1)
        first_sum(g, 0)
    for cp in list(terms_k.values()) + list(terms_v.values()):
        cp.wait_send()

    pl.semaphore_wait(greet.at[1], 1)
    along_z = {}
    for g in range(2):
        for kind in (1, 0):
            for d in range(1, NY):
                second[g, kind, d].wait_recv()
            for p in range(2):
                total = acc[g, kind, y if kind == 0 else 0, p]
                for d in range(1, NY):
                    total += yr[g, kind, d, p].astype(jnp.float32)
                zs[g, 4 * p + 2 * kind] = total[0:16]
                zs[g, 4 * p + 2 * kind + 1] = total[16:32]
        for d in range(1, NZ):
            src = zs.at[g, lax.rem(z + d, NZ)]
            along_z[g, d] = send(src, zr.at[g, d], z_s.at[g, d], z_r.at[g, d], at(dz=d))
    for cp in second.values():
        cp.wait_send()

    for g in range(2):
        total = zs[g, z]
        for d in range(1, NZ):
            along_z[g, d].wait_recv()
            total += zr[g, d]
        fin[y, z, g] = total.astype(jnp.bfloat16)
    here = fin.at[y, z]
    back_z = [send(here, here, za_s.at[d], za_r.at[d], at(dz=d)) for d in range(1, NZ)]
    for cp in along_z.values():
        cp.wait_send()
    for cp in outs:
        cp.wait()
    for cp in back_z:
        cp.wait_recv()
    here = fin.at[y]
    back_y = [send(here, here, ya_s.at[d], ya_r.at[d], at(dy=d)) for d in range(1, NY)]
    for cp in back_z:
        cp.wait_send()
    for cp in back_y:
        cp.wait_recv()
    last = local(fin, fin_hbm, out_s.at[3])
    for cp in back_y:
        cp.wait_send()
    last.wait()


def hand_over(gq_in, gbk_in, gbv_in, fin, gq_ref, gbk_ref, gbv_ref, gpk_ref, gpv_ref):
    gq_ref[...] = gq_in[...]
    gbk_ref[...] = gbk_in[...]
    gbv_ref[...] = gbv_in[...]
    for g in range(2):
        cols = pl.ds(g * HDIM, HDIM)
        for quarter in range(NY):
            for p in range(2):
                for low in range(2):
                    row = pl.ds(quarter * ROWS + low * 16, 16)
                    gpk_ref[p, row, cols] = fin[quarter, 4 * p + low, g]
                    gpv_ref[p, row, cols] = fin[quarter, 4 * p + 2 + low, g]


def body(queries, branch_keys, branch_values, grad_out, prefix_keys, prefix_values, branch_prefix, branch_blocks):
    bf16, f32 = jnp.bfloat16, jnp.float32
    smem = pl.BlockSpec(memory_space=pltpu.SMEM)
    hbm = pl.BlockSpec(memory_space=pltpu.HBM)
    anywhere = pl.BlockSpec(memory_space=pl.ANY)
    width = GROUP * BLK
    dma = pltpu.SemaphoreType.DMA
    shapes = [a.shape for a in (queries, branch_keys, branch_values, prefix_keys, prefix_values)]
    wide, narrow = (pltpu.VMEM(shape, bf16) for shape in shapes[:2])
    out_shape = [jax.ShapeDtypeStruct(shape, bf16) for shape in shapes]
    results = pl.pallas_call(
        kernel,
        out_shape=out_shape[:3] + [jax.ShapeDtypeStruct((NY, NZ, 2, 16, HDIM), bf16)],
        in_specs=[smem, smem] + [hbm] * 6,
        out_specs=[anywhere] * 4,
        scratch_shapes=[
            wide,
            narrow,
            narrow,
            wide,
            wide,
            narrow,
            narrow,
            pltpu.VMEM((2, 2, NX, 2, BLK, HDIM), bf16),
            pltpu.VMEM((2, 2, NX, NY, 2, ROWS, HDIM), bf16),
            pltpu.VMEM((2, OWNERS, BLK, HDIM), bf16),
            pltpu.VMEM((2, width, HDIM), bf16),
            pltpu.VMEM((2, width, HDIM), bf16),
            pltpu.VMEM((2, OWNERS + 1, BLK, width), f32),
            pltpu.VMEM((2, OWNERS + 1, BLK, width), f32),
            pltpu.VMEM((2, OWNERS + 1, BLK, width), bf16),
            pltpu.VMEM((2, OWNERS + 1, BLK, width), bf16),
            pltpu.VMEM((2, NX, NY, ROWS, HDIM), f32),
            pltpu.VMEM((2, BLK, HDIM), f32),
            pltpu.VMEM((2, BLK, HDIM), f32),
        ]
        + [pltpu.VMEM((2, len(RELS), BLK + 16, HDIM), bf16)] * 4
        + [
            pltpu.VMEM((2, 2, NY, 2, ROWS, HDIM), f32),
            pltpu.VMEM((2, 2, NY, 2, ROWS, HDIM), bf16),
            pltpu.VMEM((2, 2, NY, 2, ROWS, HDIM), bf16),
            pltpu.VMEM((2, NZ, 16, HDIM), f32),
            pltpu.VMEM((2, NZ, 16, HDIM), f32),
            pltpu.VMEM((NY, NZ, 2, 16, HDIM), bf16),
        ]
        + [dma((2, NX))] * 8
        + [dma((2, NY + 1))] * 2
        + [dma((2, len(RELS)))] * 4
        + [dma((2, 2, NY))] * 2
        + [dma((2, NZ))] * 2
        + [dma((NZ,))] * 2
        + [dma((NY,))] * 2
        + [dma((2 * NY + 6,)), dma((4,)), pltpu.SemaphoreType.REGULAR((2,))],
        compiler_params=pltpu.CompilerParams(
            collective_id=0, has_side_effects=True, vmem_limit_bytes=63 << 20
        ),
        name="attention_backward",
    )(branch_prefix, branch_blocks, queries, branch_keys, branch_values, grad_out, prefix_keys, prefix_values)
    return pl.pallas_call(
        hand_over,
        out_shape=out_shape,
        in_specs=[pl.BlockSpec(memory_space=pltpu.VMEM)] * 4,
        out_specs=[pl.BlockSpec(memory_space=pltpu.VMEM)] * 5,
        name="hand_over",
    )(*results)


def solution(mesh):
    split = P(("prefix", "branch"), None, "tensor")
    rows = P(None, "prefix", "tensor")
    ids = P(("prefix", "branch"))
    return jax.shard_map(
        body,
        mesh=mesh,
        in_specs=(split, split, split, split, rows, rows, ids, ids),
        out_specs=(split, split, split, rows, rows),
        check_vma=False,
    )
```
